128 devices in a mesh: row: 2 (over y_lo), col: 8 (over x, core), layer: 8 (over y_hi, z).
Axes of the slice: x: 4, y: 4 (y_hi: 2, y_lo: 2; y = y_hi * 2 + y_lo), z: 4, core: 2. Of those that a mesh axis runs over, the one named last changes fastest.
Arguments:
- left: float32 [1024, 8192], P('row', ('layer', 'col')), may hold values from -6 to 6
- right: float32 [8192, 16384], P(('layer', 'row'), 'col'), may hold values from -0.125 to 0.125
- left_mask: int32 [2, 16], replicated, may hold values 0 or 1
- right_mask: int32 [16, 32], replicated, may hold values 0 or 1
- result_mask: int32 [2, 32], replicated, may hold values 0 or 1
Outputs:
- ladder: float32 [1024, 16384], P('row', ('col', 'layer'))
The draws below stay inside these ranges and needn't reach their ends.
Inputs may be any that keep to these rules, and one draw needn't show every extreme that they name: `left_mask`: 1 marks a present tile, 0 an absent one. `right_mask`: 1 marks a present tile, 0 an absent one. `result_mask`: 1 marks a present tile, 0 an absent one.
All inputs are finite; a program needn't handle non-finite values.
Results may differ from the reference program's by a relative error of at most 0.0003.
Values sent between devices are 32-bit elements; how exact they have to be, the bound alone decides.
No kernel may reach another device: no remote copies, remote signals or barrier semaphores. Data moves between devices by JAX's collectives and lax.ppermute only.
A program may use at most 64 MiB of HBM per device.

```python
import jax
import jax.numpy as jnp
from jax import lax

K = 8192
N = 16384
TILE = 512
M = 1024
MT = 2
KT = 16
NT = 32


def place_ends(array, stream_key, low, largest):
    longest = array.shape.index(max(array.shape))
    spots = []
    for shift in (0, 1):
        where = [jax.random.randint(jax.random.fold_in(stream_key, axis), (), 0, length) for axis, length in enumerate(array.shape)]
        where[longest] = (where[longest] + shift) % array.shape[longest]
        spots.append(tuple(where))
    return array.at[spots[0]].set(low).at[spots[1]].set(largest)


def shard_levels(own_key, shape, shards, low, top_value):
    loudness = 1.0
    for dim, parts in shards:
        heights = jax.random.uniform(jax.random.fold_in(jax.random.fold_in(own_key, 6), dim), (parts,), jnp.float32, low / len(shards), top_value / len(shards))
        loudness = loudness * jnp.repeat(jnp.exp(heights), shape[dim] // parts).reshape((-1,) + (1,) * (len(shape) - 1 - dim))
    return loudness


def gaussian(key, extent, spread, bound, pieces=(), kind=jnp.bfloat16):
    loudness = shard_levels(key, extent, pieces, -0.22, 0.18) if pieces else 1.0
    result = jax.random.normal(key, extent, jnp.float32) * spread * loudness
    return jnp.minimum(jnp.maximum(result, -bound), bound).astype(kind)


def setup_inputs(seed: int = 0) -> dict:
    arg_keys = jax.random.split(jax.random.key(seed), 6)
    left = gaussian(arg_keys[0], (M, K), 1.0, 6.0, ((0, 2), (1, 64)), jnp.float32)
    right = gaussian(arg_keys[1], (K, N), (K // 4) ** -0.5, 0.125, ((0, 16), (1, 8)), jnp.float32)
    left_mask = place_ends((jax.random.randint(arg_keys[2], (MT, KT), 0, 2) < 1).astype(jnp.int32), jax.random.fold_in(arg_keys[2], 1), 0, 1)
    right_mask = place_ends((jax.random.randint(arg_keys[3], (KT, NT), 0, 2) < 1).astype(jnp.int32), jax.random.fold_in(arg_keys[3], 1), 0, 1)
    result_mask = place_ends((jax.random.randint(arg_keys[4], (MT, NT), 0, 2) < 1).astype(jnp.int32), jax.random.fold_in(arg_keys[4], 1), 0, 1)
    return dict(left=left, right=right, left_mask=left_mask, right_mask=right_mask, result_mask=result_mask)


def reference(left, right, left_mask, right_mask, result_mask):
    rows_total = left.shape[0]
    tile_rows = left_mask.shape[0]
    tile_inner = right_mask.shape[0]
    tile_cols = right_mask.shape[1]
    padded = jnp.pad(left, ((0, tile_rows * TILE - rows_total), (0, 0)))

    def column(jcol):
        def per_row(irow):
            def step(kidx, total):
                kpos = jnp.asarray(kidx).astype(jnp.int32)
                usable = (left_mask[irow, kpos] * right_mask[kpos, jcol] * result_mask[irow, jcol]) > 0
                block_a = lax.dynamic_slice(padded, ((irow * TILE).astype(jnp.int32), (kpos * TILE).astype(jnp.int32)), (TILE, TILE))
                block_b = lax.dynamic_slice(right, ((kpos * TILE).astype(jnp.int32), (jcol * TILE).astype(jnp.int32)), (TILE, TILE))
                return lax.cond(usable, lambda acc: acc + jnp.dot(block_a, block_b, precision=lax.Precision.HIGHEST), lambda acc: acc, total)
            return lax.fori_loop(0, tile_inner, step, jnp.zeros((TILE, TILE), left.dtype))
        return lax.map(per_row, jnp.arange(tile_rows, dtype=jnp.int32))

    blocks = lax.map(column, jnp.arange(tile_cols, dtype=jnp.int32))
    whole = jnp.transpose(blocks, (1, 2, 0, 3)).reshape(tile_rows * TILE, tile_cols * TILE)
    return whole[:rows_total]
```

```python
import jax
import jax.numpy as jnp
from jax import lax
from jax.experimental import pallas as pl
from jax.experimental.pallas import tpu as pltpu
from jax.sharding import Mesh
from jax.sharding import PartitionSpec as P

TILE = 512
PART = 256
AXES = ("yl", "x", "c", "yh", "z")
SIZES = (2, 4, 2, 2, 4)
UP, DOWN = (1, 2), (0, 3)
OWN_ROW, OTHER_ROW = (0, 2), (1, 3)


def everyone():
    for yl in range(2):
        for x in range(4):
            for c in range(2):
                for yh in range(2):
                    for z in range(4):
                        yield yl, x, c, yh, z


def number(yl, x, c, yh, z):
    return (((yl * 4 + x) * 2 + c) * 2 + yh) * 4 + z


def permute(value, target):
    pairs = []
    for place in everyone():
        there = target(*place)
        if there is not None:
            pairs.append((number(*place), number(*there)))
    return lax.ppermute(value, AXES, pairs)


def along_y(value, step):
    def target(yl, x, c, yh, z):
        y = (2 * yh + yl + step) % 4
        return y % 2, x, c, y // 2, z

    return permute(value, target)


def along_z(value, step):
    return permute(value, lambda yl, x, c, yh, z: (yl, x, c, yh, (z + step) % 4))


def swap_cores(value):
    return permute(value, lambda yl, x, c, yh, z: (yl, x, 1 - c, yh, z))


def swap_rows(value):
    def target(yl, x, c, yh, z):
        return (1 - yl, x, c, yh, z) if x // 2 != yl else None

    return permute(value, target)


def spread(value, yl, x):
    def up(yl, x, c, yh, z):
        return (yl, (x + 1) % 4, c, yh, z) if x // 2 == yl else None

    def down(yl, x, c, yh, z):
        return (yl, (x - 1) % 4, c, yh, z) if x // 2 == yl else None

    def across(yl, x, c, yh, z):
        return (yl, (x + 2) % 4, c, yh, z) if x // 2 == yl else None

    from_below = permute(value, up)
    from_above = permute(value, down)
    from_across = permute(value, across)
    place = (x - 2 * yl) % 4
    low = jnp.where(
        place == 0, value, jnp.where(place == 1, from_below, jnp.where(place == 2, from_across, from_above))
    )
    high = jnp.where(
        place == 1, value, jnp.where(place == 0, from_above, jnp.where(place == 2, from_below, from_across))
    )
    return jnp.stack([low, high])


def product_kernel(turns, plan, spots, left_mask, right_mask, result_mask, mine, other, right, *rest):
    outs, (hi_ref, lo_ref) = rest[:-2], rest[-2:]
    yl, x, c, yh, z = (spots[n] for n in range(5))
    y = 2 * yh + yl
    k = (yh * 4 + z) * 2 + yl
    first = (x * 2 + c) * 4
    for s in range(2):
        for block, core in ((mine, c), (other, 1 - c)):
            piece = block[s]
            hi = piece.astype(jnp.bfloat16)
            where = pl.ds(pl.multiple_of(s * 256 + core * 128, 128), 128)
            hi_ref[:, where] = hi
            lo_ref[:, where] = (piece - hi.astype(jnp.float32)).astype(jnp.bfloat16)
    for dy in turns:
        there = lax.rem(y + dy, 4)
        i, half = lax.rem(there, 2), lax.div(there, 2)
        for dz in range(4):
            chunk = half * 4 + lax.rem(z + dz, 4)
            j = first + lax.div(chunk, 2)
            used = left_mask[i, k] * right_mask[k, j] * result_mask[i, j]
            (top, t), (bottom, b) = plan[dy, dz]

            @pl.when(used > 0)
            def _():
                tile = right[:, pl.ds(pl.multiple_of(chunk * 256, 256), 256)]
                hi = tile.astype(jnp.bfloat16)
                lo = (tile - hi.astype(jnp.float32)).astype(jnp.bfloat16)
                total = jnp.dot(hi_ref[...], hi, preferred_element_type=jnp.float32)
                total += jnp.dot(hi_ref[...], lo, preferred_element_type=jnp.float32)
                total += jnp.dot(lo_ref[...], hi, preferred_element_type=jnp.float32)
                outs[top][t] = total[:PART]
                outs[bottom][b] = total[PART:]

            @pl.when(used == 0)
            def _():
                outs[top][t] = jnp.zeros((PART, 256), jnp.float32)
                outs[bottom][b] = jnp.zeros((PART, 256), jnp.float32)


def product(turns, names, spots, masks, mine, right):
    plan = {}
    for dy in turns:
        for dz in range(4):
            slots = []
            for half in "AB":
                for n, blocks in enumerate(names.values()):
                    if (half, dy, dz) in blocks:
                        slots.append((n, blocks.index((half, dy, dz))))
            plan[dy, dz] = slots
    smem = pl.BlockSpec(memory_space=pltpu.SMEM)
    vmem = pl.BlockSpec(memory_space=pltpu.VMEM)
    outs = pl.pallas_call(
        lambda *refs: product_kernel(turns, plan, *refs),
        out_shape=[jax.ShapeDtypeStruct((len(b), PART, 256), jnp.float32) for b in names.values()],
        in_specs=[smem] * 4 + [vmem] * 3,
        out_specs=[vmem] * len(names),
        scratch_shapes=[pltpu.VMEM((TILE, TILE), jnp.bfloat16)] * 2,
        compiler_params=pltpu.CompilerParams(vmem_limit_bytes=32 * 2**20),
        cost_estimate=pl.CostEstimate(
            flops=3 * 2 * TILE * TILE * 2048, bytes_accessed=9 * 2**20, transcendentals=0
        ),
    )(spots, *masks, mine, swap_cores(mine), right)
    return dict(zip(names, outs))


def shards(left, right, left_mask, right_mask, result_mask):
    yl, x, c, yh, z = (lax.axis_index(a) for a in AXES)
    spots = jnp.stack([yl, x, c, yh, z]).astype(jnp.int32)
    masks = (left_mask, right_mask, result_mask)

    mine = spread(left, yl, x)
    theirs = spread(swap_rows(left), yl, x)
    p = product(
        OWN_ROW,
        {
            "a1_up": [("A", 2, d) for d in UP],
            "a1_down": [("A", 2, d) for d in DOWN],
            "b1_up": [("B", d, 2) for d in OWN_ROW],
            "b2_down": [("B", d, 3) for d in OWN_ROW],
            "b3_up": [("B", d, 1) for d in OWN_ROW],
            "a_up": [("A", 0, d) for d in UP],
            "a_down": [("A", 0, d) for d in DOWN],
            "b_own": [("B", d, 0) for d in OWN_ROW],
        },
        spots,
        masks,
        mine,
        right,
    )
    a1_up = along_y(p["a1_up"], 1)
    a1_down = along_y(p["a1_down"], -1)
    b1_up = along_z(p["b1_up"], 1)
    b2_down = along_z(p["b2_down"], -1)
    q = product(
        OTHER_ROW,
        {
            "a2_up": [("A", 1, d) for d in DOWN],
            "a2_down": [("A", 3, d) for d in UP],
            "b1_down": [("B", d, 2) for d in OTHER_ROW],
            "b2_up": [("B", d, 1) for d in OTHER_ROW],
            "a3_up": [("A", 1, d) for d in UP],
            "a3_down": [("A", 3, d) for d in DOWN],
            "b3_down": [("B", d, 3) for d in OTHER_ROW],
            "b_other": [("B", d, 0) for d in OTHER_ROW],
        },
        spots,
        masks,
        theirs,
        right,
    )
    b1_down = along_z(q["b1_down"], -1)
    a2_up = along_y(q["a2_up"], 1)
    a2_down = along_y(q["a2_down"], -1)
    b2_up = along_z(q["b2_up"], 1)
    a3_up = along_y(q["a3_up"] + a1_up, 1)
    a3_down = along_y(q["a3_down"] + a1_down, -1)
    b3_up = along_z(p["b3_up"] + b1_up, 1)
    b3_down = along_z(q["b3_down"] + b1_down, -1)
    a = dict(zip(UP, p["a_up"] + a2_down + a3_up)) | dict(zip(DOWN, p["a_down"] + a2_up + a3_down))
    b = dict(zip(OWN_ROW, p["b_own"] + b2_down + b3_up)) | dict(
        zip(OTHER_ROW, q["b_other"] + b2_up + b3_down)
    )
    top = a[0] + along_z(a[1], 1) + along_z(a[2], 2) + along_z(a[3], -1)
    bottom = b[0] + along_y(b[1], 1) + along_y(b[2], 2) + along_y(b[3], -1)
    return jnp.concatenate([top, bottom])


def solution(mesh):
    torus = Mesh(mesh.devices.reshape(SIZES), AXES)
    in_specs = (
        P("yl", ("yh", "z", "x", "c")),
        P(("yh", "z", "yl"), ("x", "c")),
        P(),
        P(),
        P(),
    )
    return jax.shard_map(
        shards, mesh=torus, in_specs=in_specs, out_specs=P("yl", ("x", "c", "yh", "z")), check_vma=False
    )
```

```python
import jax
import jax.numpy as jnp
from jax import lax
from jax.experimental import pallas as pl
from jax.experimental.pallas import tpu as pltpu
from jax.sharding import Mesh
from jax.sharding import PartitionSpec as P

TILE = 512
WIDTH = 256
AXES = ("yl", "x", "c", "yh", "z")
SIZES = (2, 4, 2, 2, 4)
ROWS = {"A": 320, "B": 192}
SMEM = pl.BlockSpec(memory_space=pltpu.SMEM)
VMEM = pl.BlockSpec(memory_space=pltpu.VMEM)


def permute(value, yl=0, x=0, c=0, yh=0, z=0, senders=lambda yl, x: True):
    pairs = []
    for a in range(2):
        for b in range(4):
            if senders(a, b):
                for d in range(2):
                    for e in range(2):
                        for f in range(4):
                            pairs.append((number(a, b, d, e, f), number(a ^ yl, b ^ x, d ^ c, e ^ yh, f ^ z)))
    return lax.ppermute(value, AXES, pairs)


def number(yl, x, c, yh, z):
    return (((yl * 4 + x) * 2 + c) * 2 + yh) * 4 + z


def along_y(value, bits):
    return permute(value, yl=bits % 2, yh=bits // 2)


def along_z(value, bits):
    return permute(value, z=bits)


def source(yl, x):
    return x // 2 == yl


def split_kernel(right, hi_ref, lo_ref):
    @pl.loop(0, 2048, step=WIDTH)
    def _(start):
        where = pl.ds(pl.multiple_of(start, WIDTH), WIDTH)
        tile = right[:, where]
        hi = tile.astype(jnp.bfloat16)
        hi_ref[:, where] = hi
        lo_ref[:, where] = (tile - hi.astype(jnp.float32)).astype(jnp.bfloat16)


def split(right):
    return pl.pallas_call(
        split_kernel,
        out_shape=[jax.ShapeDtypeStruct(right.shape, jnp.bfloat16)] * 2,
        in_specs=[VMEM],
        out_specs=[VMEM] * 2,
        compiler_params=pltpu.CompilerParams(vmem_limit_bytes=32 * 2**20),
        cost_estimate=pl.CostEstimate(flops=3 * right.size, bytes_accessed=8 * right.size, transcendentals=0),
    )(right)


def product_kernel(rows, plan, spots, left_mask, right_mask, result_mask, *rest):
    pieces, (right_hi, right_lo), outs, (hi_ref, lo_ref) = rest[:4], rest[4:6], rest[6:-2], rest[-2:]
    yl, x, c, yh, z = (spots[n] for n in range(5))
    k = (yh * 4 + z) * 2 + yl
    first = (x * 2 + c) * 4
    near = 1 - lax.rem(x, 2)
    for piece, chip, core in zip(pieces, (near, 1 - near, near, 1 - near), (c, c, 1 - c, 1 - c)):
        value = piece[...]
        hi = value.astype(jnp.bfloat16)
        where = pl.ds(pl.multiple_of(chip * 256 + core * 128, 128), 128)
        hi_ref[:, where] = hi
        lo_ref[:, where] = (value - hi.astype(jnp.float32)).astype(jnp.bfloat16)
    for dy, (start, stop) in rows.items():
        i = lax.rem(yl + dy % 2, 2)
        half = lax.rem(yh + dy // 2, 2)
        for dz in range(4):
            chunk = half * 4 + jnp.bitwise_xor(z, dz)
            j = first + lax.div(chunk, 2)
            used = left_mask[i, k] * right_mask[k, j] * result_mask[i, j]

            @pl.when(used > 0)
            def _():
                where = pl.ds(pl.multiple_of(chunk * WIDTH, WIDTH), WIDTH)
                hi, lo = right_hi[:, where], right_lo[:, where]
                total = jnp.dot(hi_ref[start:stop], hi, preferred_element_type=jnp.float32)
                total += jnp.dot(hi_ref[start:stop], lo, preferred_element_type=jnp.float32)
                total += jnp.dot(lo_ref[start:stop], hi, preferred_element_type=jnp.float32)
                done = 0
                for half, n, slot in plan[dy, dz]:
                    outs[n][slot] = total[done : done + ROWS[half]]
                    done += ROWS[half]

            @pl.when(used == 0)
            def _():
                for half, n, slot in plan[dy, dz]:
                    outs[n][slot] = jnp.zeros((ROWS[half], WIDTH), jnp.float32)


def product(rows, names, spots, masks, pieces, right):
    plan = {
        (dy, dz): [
            (half, n, blocks.index((half, dy, dz)))
            for half in "AB"
            for n, blocks in enumerate(names.values())
            if (half, dy, dz) in blocks
        ]
        for dy in rows
        for dz in range(4)
    }
    work = 3 * 2 * TILE * WIDTH * 4 * sum(stop - start for start, stop in rows.values())
    outs = pl.pallas_call(
        lambda *refs: product_kernel(rows, plan, *refs),
        out_shape=[jax.ShapeDtypeStruct((len(b), ROWS[b[0][0]], WIDTH), jnp.float32) for b in names.values()],
        in_specs=[SMEM] * 4 + [VMEM] * 6,
        out_specs=[VMEM] * len(names),
        scratch_shapes=[pltpu.VMEM((pieces[0].shape[0], TILE), jnp.bfloat16)] * 2,
        compiler_params=pltpu.CompilerParams(vmem_limit_bytes=32 * 2**20),
        cost_estimate=pl.CostEstimate(flops=work, bytes_accessed=4 * 2**20, transcendentals=0),
    )(spots, *masks, *pieces, *right)
    return dict(zip(names, outs))


def join(value, first, arrived):
    def kernel(value_ref, arrived_ref, out_ref):
        del value_ref
        for n in range(arrived.shape[0]):
            out_ref[first + n] += arrived_ref[n]

    return pl.pallas_call(
        kernel,
        out_shape=jax.ShapeDtypeStruct(value.shape, value.dtype),
        in_specs=[VMEM] * 2,
        out_specs=VMEM,
        input_output_aliases={0: 0},
        compiler_params=pltpu.CompilerParams(vmem_limit_bytes=32 * 2**20),
        cost_estimate=pl.CostEstimate(flops=arrived.size, bytes_accessed=12 * arrived.size, transcendentals=0),
    )(value, arrived)


def gather(value, here):
    between, beside, across = (permute(value, x=bits, senders=source) for bits in (1, 3, 2))
    near = jnp.where(here, between, beside)
    far = jnp.where(here, value, across)
    return near, far


def both_cores(near, far):
    return near, far, permute(near, c=1), permute(far, c=1)


def shards(left, right, left_mask, right_mask, result_mask):
    yl, x, c, yh, z = (lax.axis_index(a) for a in AXES)
    spots = jnp.stack([yl, x, c, yh, z]).astype(jnp.int32)
    masks = (left_mask, right_mask, result_mask)
    here = source(yl, x)
    rows_a = ROWS["A"]

    own = gather(left[:rows_a], here)
    other_row = permute(left, yl=1, senders=lambda yl, x: not source(yl, x))
    rest = gather(jnp.concatenate([left[rows_a:], other_row]), here)
    right = split(right)
    p = product(
        {0: (0, rows_a), 2: (0, rows_a)},
        {
            "via1": [("A", 2, 0), ("A", 2, 1)],
            "via3": [("A", 2, 2), ("A", 2, 3)],
            "own": [("A", 0, d) for d in range(4)],
        },
        spots,
        masks,
        both_cores(*own),
        right,
    )
    from1 = along_y(p["via1"], 1)
    from3 = along_y(p["via3"], 3)
    rest, a_own = lax.optimization_barrier((rest, p["own"]))
    own_rows, other_rows = (0, ROWS["B"]), (ROWS["B"], ROWS["B"] + TILE)
    q = product(
        {1: other_rows, 3: other_rows, 0: own_rows, 2: own_rows},
        {
            "a1": [("A", 1, d) for d in range(4)],
            "a3": [("A", 3, d) for d in range(4)],
            "via1": [("B", 0, 2), ("B", 1, 2)],
            "via3": [("B", 2, 2), ("B", 3, 2)],
            "b1": [("B", d, 1) for d in range(4)],
            "b3": [("B", d, 3) for d in range(4)],
            "own": [("B", d, 0) for d in range(4)],
        },
        spots,
        masks,
        both_cores(*rest),
        right,
    )
    top_parts = (along_y(join(q["a1"], 2, from3), 1), along_y(join(q["a3"], 0, from1), 3))
    from1 = along_z(q["via1"], 1)
    from3 = along_z(q["via3"], 3)
    bottom_parts = (along_z(join(q["b1"], 2, from3), 1), along_z(join(q["b3"], 0, from1), 3))

    a = [a_own[d] + top_parts[0][d] + top_parts[1][d] for d in range(4)]
    b = [q["own"][d] + bottom_parts[0][d] + bottom_parts[1][d] for d in range(4)]
    top = a[0] + along_z(a[2], 2) + along_z(a[1], 1) + along_z(a[3], 3)
    bottom = b[0] + along_y(b[2], 2) + along_y(b[1], 1) + along_y(b[3], 3)
    return jnp.concatenate([top, bottom])


def solution(mesh):
    torus = Mesh(mesh.devices.reshape(SIZES), AXES)
    in_specs = (
        P("yl", ("yh", "z", "x", "c")),
        P(("yh", "z", "yl"), ("x", "c")),
        P(),
        P(),
        P(),
    )
    return jax.shard_map(
        shards, mesh=torus, in_specs=in_specs, out_specs=P("yl", ("x", "c", "yh", "z")), check_vma=False
    )
```

```python
import jax
import jax.numpy as jnp
from jax import lax
from jax.experimental import pallas as pl
from jax.experimental.pallas import tpu as pltpu
from jax.sharding import Mesh
from jax.sharding import PartitionSpec as P

TILE = 512
WIDTH = 256
AXES = ("yl", "x", "c", "yh", "z")
SIZES = (2, 4, 2, 2, 4)
ROWS = {"A": 320, "B": 192}
SMEM = pl.BlockSpec(memory_space=pltpu.SMEM)
VMEM = pl.BlockSpec(memory_space=pltpu.VMEM)


def permute(value, yl=0, x=0, c=0, yh=0, z=0, senders=lambda yl, x: True):
    pairs = []
    for a in range(2):
        for b in range(4):
            if senders(a, b):
                for d in range(2):
                    for e in range(2):
                        for f in range(4):
                            pairs.append((number(a, b, d, e, f), number(a ^ yl, b ^ x, d ^ c, e ^ yh, f ^ z)))
    return lax.ppermute(value, AXES, pairs)


def number(yl, x, c, yh, z):
    return (((yl * 4 + x) * 2 + c) * 2 + yh) * 4 + z


def along_y(value, bits):
    return permute(value, yl=bits % 2, yh=bits // 2)


def along_z(value, bits):
    return permute(value, z=bits)


def source(yl, x):
    return x // 2 == yl


def split_kernel(right, hi_ref, lo_ref):
    @pl.loop(0, 2048, step=WIDTH)
    def _(start):
        where = pl.ds(pl.multiple_of(start, WIDTH), WIDTH)
        tile = right[:, where]
        hi = tile.astype(jnp.bfloat16)
        hi_ref[:, where] = hi
        lo_ref[:, where] = (tile - hi.astype(jnp.float32)).astype(jnp.bfloat16)


def split(right):
    return pl.pallas_call(
        split_kernel,
        out_shape=[jax.ShapeDtypeStruct(right.shape, jnp.bfloat16)] * 2,
        in_specs=[VMEM],
        out_specs=[VMEM] * 2,
        compiler_params=pltpu.CompilerParams(vmem_limit_bytes=32 * 2**20),
        cost_estimate=pl.CostEstimate(flops=1, bytes_accessed=1, transcendentals=0),
    )(right)


def product_kernel(rows, plan, spots, left_mask, right_mask, result_mask, *rest):
    pieces, (right_hi, right_lo), outs, (hi_ref, lo_ref) = rest[:4], rest[4:6], rest[6:-2], rest[-2:]
    yl, x, c, yh, z = (spots[n] for n in range(5))
    k = (yh * 4 + z) * 2 + yl
    first = (x * 2 + c) * 4
    near = 1 - lax.rem(x, 2)
    for piece, chip, core in zip(pieces, (near, 1 - near, near, 1 - near), (c, c, 1 - c, 1 - c)):
        value = piece[...]
        hi = value.astype(jnp.bfloat16)
        where = pl.ds(pl.multiple_of(chip * 256 + core * 128, 128), 128)
        hi_ref[:, where] = hi
        lo_ref[:, where] = (value - hi.astype(jnp.float32)).astype(jnp.bfloat16)
    for dy, (start, stop) in rows.items():
        i = lax.rem(yl + dy % 2, 2)
        half = lax.rem(yh + dy // 2, 2)
        for dz in range(4):
            chunk = half * 4 + jnp.bitwise_xor(z, dz)
            j = first + lax.div(chunk, 2)
            used = left_mask[i, k] * right_mask[k, j] * result_mask[i, j]

            @pl.when(used > 0)
            def _():
                where = pl.ds(pl.multiple_of(chunk * WIDTH, WIDTH), WIDTH)
                hi, lo = right_hi[:, where], right_lo[:, where]
                total = jnp.dot(hi_ref[start:stop], hi, preferred_element_type=jnp.float32)
                total += jnp.dot(hi_ref[start:stop], lo, preferred_element_type=jnp.float32)
                total += jnp.dot(lo_ref[start:stop], hi, preferred_element_type=jnp.float32)
                done = 0
                for half, n, slot in plan[dy, dz]:
                    outs[n][slot] = total[done : done + ROWS[half]]
                    done += ROWS[half]

            @pl.when(used == 0)
            def _():
                for half, n, slot in plan[dy, dz]:
                    outs[n][slot] = jnp.zeros((ROWS[half], WIDTH), jnp.float32)


def product(rows, names, spots, masks, pieces, right):
    plan = {
        (dy, dz): [
            (half, n, blocks.index((half, dy, dz)))
            for half in "AB"
            for n, blocks in enumerate(names.values())
            if (half, dy, dz) in blocks
        ]
        for dy in rows
        for dz in range(4)
    }
    work = 3 * 2 * TILE * WIDTH * 4 * sum(stop - start for start, stop in rows.values())
    outs = pl.pallas_call(
        lambda *refs: product_kernel(rows, plan, *refs),
        out_shape=[jax.ShapeDtypeStruct((len(b), ROWS[b[0][0]], WIDTH), jnp.float32) for b in names.values()],
        in_specs=[SMEM] * 4 + [VMEM] * 6,
        out_specs=[VMEM] * len(names),
        scratch_shapes=[pltpu.VMEM((pieces[0].shape[0], TILE), jnp.bfloat16)] * 2,
        compiler_params=pltpu.CompilerParams(vmem_limit_bytes=32 * 2**20),
        cost_estimate=pl.CostEstimate(flops=1, bytes_accessed=1, transcendentals=0),
    )(spots, *masks, *pieces, *right)
    return dict(zip(names, outs))


def join(value, first, arrived):
    def kernel(value_ref, arrived_ref, out_ref):
        del value_ref
        for n in range(arrived.shape[0]):
            out_ref[first + n] += arrived_ref[n]

    return pl.pallas_call(
        kernel,
        out_shape=jax.ShapeDtypeStruct(value.shape, value.dtype),
        in_specs=[VMEM] * 2,
        out_specs=VMEM,
        input_output_aliases={0: 0},
        compiler_params=pltpu.CompilerParams(vmem_limit_bytes=32 * 2**20),
        cost_estimate=pl.CostEstimate(flops=1, bytes_accessed=1, transcendentals=0),
    )(value, arrived)


def gather(value, here):
    between, beside, across = (permute(value, x=bits, senders=source) for bits in (1, 3, 2))
    near = jnp.where(here, between, beside)
    far = jnp.where(here, value, across)
    return near, far


def both_cores(near, far):
    return near, far, permute(near, c=1), permute(far, c=1)


def shards(left, right, left_mask, right_mask, result_mask):
    yl, x, c, yh, z = (lax.axis_index(a) for a in AXES)
    spots = jnp.stack([yl, x, c, yh, z]).astype(jnp.int32)
    masks = (left_mask, right_mask, result_mask)
    here = source(yl, x)
    rows_a = ROWS["A"]

    own = gather(left[:rows_a], here)
    other_row = permute(left, yl=1, senders=lambda yl, x: not source(yl, x))
    rest = gather(jnp.concatenate([left[rows_a:], other_row]), here)
    right = split(right)
    p = product(
        {0: (0, rows_a), 2: (0, rows_a)},
        {
            "via1": [("A", 2, 0), ("A", 2, 1)],
            "via3": [("A", 2, 2), ("A", 2, 3)],
            "own": [("A", 0, d) for d in range(4)],
        },
        spots,
        masks,
        both_cores(*own),
        right,
    )
    from1 = along_y(p["via1"], 1)
    from3 = along_y(p["via3"], 3)
    rest, a_own = lax.optimization_barrier((rest, p["own"]))
    own_rows, other_rows = (0, ROWS["B"]), (ROWS["B"], ROWS["B"] + TILE)
    q = product(
        {1: other_rows, 3: other_rows, 0: own_rows, 2: own_rows},
        {
            "a1": [("A", 1, d) for d in range(4)],
            "a3": [("A", 3, d) for d in range(4)],
            "via1": [("B", 0, 2), ("B", 1, 2)],
            "via3": [("B", 2, 2), ("B", 3, 2)],
            "b1": [("B", d, 1) for d in range(4)],
            "b3": [("B", d, 3) for d in range(4)],
            "own": [("B", d, 0) for d in range(4)],
        },
        spots,
        masks,
        both_cores(*rest),
        right,
    )
    top_parts = (along_y(join(q["a1"], 2, from3), 1), along_y(join(q["a3"], 0, from1), 3))
    from1 = along_z(q["via1"], 1)
    from3 = along_z(q["via3"], 3)
    bottom_parts = (along_z(join(q["b1"], 2, from3), 1), along_z(join(q["b3"], 0, from1), 3))

    a = [a_own[d] + top_parts[0][d] + top_parts[1][d] for d in range(4)]
    b = [q["own"][d] + bottom_parts[0][d] + bottom_parts[1][d] for d in range(4)]
    top = a[0] + along_z(a[2], 2) + along_z(a[1], 1) + along_z(a[3], 3)
    bottom = b[0] + along_y(b[2], 2) + along_y(b[1], 1) + along_y(b[3], 3)
    return jnp.concatenate([top, bottom])


def solution(mesh):
    torus = Mesh(mesh.devices.reshape(SIZES), AXES)
    in_specs = (
        P("yl", ("yh", "z", "x", "c")),
        P(("yh", "z", "yl"), ("x", "c")),
        P(),
        P(),
        P(),
    )
    return jax.shard_map(
        shards, mesh=torus, in_specs=in_specs, out_specs=P("yl", ("x", "c", "yh", "z")), check_vma=False
    )
```

```python
import jax
import jax.numpy as jnp
from jax import lax
from jax.experimental import pallas as pl
from jax.experimental.pallas import tpu as pltpu
from jax.sharding import Mesh
from jax.sharding import PartitionSpec as P

TILE = 512
WIDTH = 256
AXES = ("yl", "x", "c", "yh", "z")
SIZES = (2, 4, 2, 2, 4)
ROWS = {"A": 320, "B": 192}
COST = {"first": 1, "second": 1, "join_a": 1, "join_b": 1, "last": 1}
SMEM = pl.BlockSpec(memory_space=pltpu.SMEM)
VMEM = pl.BlockSpec(memory_space=pltpu.VMEM)


def permute(value, yl=0, x=0, c=0, yh=0, z=0):
    bits = (((yl * 4 + x) * 2 + c) * 2 + yh) * 4 + z
    return lax.ppermute(value, AXES, [(n, n ^ bits) for n in range(128)])


def along_y(value, bits):
    return permute(value, yl=bits % 2, yh=bits // 2)


def along_z(value, bits):
    return permute(value, z=bits)


def settings(cost):
    return dict(
        compiler_params=pltpu.CompilerParams(vmem_limit_bytes=16 * 2**20),
        cost_estimate=pl.CostEstimate(flops=1, bytes_accessed=COST[cost], transcendentals=0),
    )


def product_kernel(rows, plan, spots, left_mask, right_mask, result_mask, *rest):
    pieces, right, outs, (hi_ref, lo_ref, tiles, sems) = rest[:4], rest[4], rest[5:-4], rest[-4:]
    yl, x, c, yh, z = (spots[n] for n in range(5))
    k = (yh * 4 + z) * 2 + yl
    first = (x * 2 + c) * 4
    near = 1 - lax.rem(x, 2)

    def used(dy, chunk):
        i = lax.rem(yl + dy % 2, 2)
        j = first + lax.div(chunk, 2)
        return left_mask[i, k] * right_mask[k, j] * result_mask[i, j] > 0

    def fetch(n, chunk):
        where = pl.ds(pl.multiple_of(chunk * WIDTH, WIDTH), WIDTH)
        return pltpu.make_async_copy(right.at[:, where], tiles.at[n], sems.at[n])

    groups = [
        (n, lax.rem(yh + high, 2) * 4 + jnp.bitwise_xor(z, dz), [dy for dy in rows if dy // 2 == high], dz)
        for n, (high, dz) in enumerate((high, dz) for high in range(2) for dz in range(4))
    ]

    def wanted(chunk, turns):
        flag = used(turns[0], chunk)
        for dy in turns[1:]:
            flag = jnp.logical_or(flag, used(dy, chunk))
        return flag

    for n, chunk, turns, _ in groups:

        @pl.when(wanted(chunk, turns))
        def _():
            fetch(n, chunk).start()

    for piece, chip, core in zip(pieces, (near, 1 - near, near, 1 - near), (c, c, 1 - c, 1 - c)):
        value = piece[...]
        hi = value.astype(jnp.bfloat16)
        where = pl.ds(pl.multiple_of(chip * 256 + core * 128, 128), 128)
        hi_ref[:, where] = hi
        lo_ref[:, where] = (value - hi.astype(jnp.float32)).astype(jnp.bfloat16)
    for n, chunk, turns, dz in groups:

        @pl.when(wanted(chunk, turns))
        def _():
            fetch(n, chunk).wait()

        for dy in turns:
            start, stop = rows[dy]

            @pl.when(used(dy, chunk))
            def _():
                tile = tiles[n]
                hi = tile.astype(jnp.bfloat16)
                lo = (tile - hi.astype(jnp.float32)).astype(jnp.bfloat16)
                total = jnp.dot(hi_ref[start:stop], hi, preferred_element_type=jnp.float32)
                total += jnp.dot(hi_ref[start:stop], lo, preferred_element_type=jnp.float32)
                total += jnp.dot(lo_ref[start:stop], hi, preferred_element_type=jnp.float32)
                done = 0
                for half, out, slot in plan[dy, dz]:
                    outs[out][slot] = total[done : done + ROWS[half]]
                    done += ROWS[half]

            @pl.when(jnp.logical_not(used(dy, chunk)))
            def _():
                for half, out, slot in plan[dy, dz]:
                    outs[out][slot] = jnp.zeros((ROWS[half], WIDTH), jnp.float32)


def product(rows, names, spots, masks, pieces, right, cost):
    plan = {
        (dy, dz): [
            (half, n, blocks.index((half, dy, dz)))
            for half in "AB"
            for n, blocks in enumerate(names.values())
            if (half, dy, dz) in blocks
        ]
        for dy in rows
        for dz in range(4)
    }
    outs = pl.pallas_call(
        lambda *refs: product_kernel(rows, plan, *refs),
        out_shape=[jax.ShapeDtypeStruct((len(b), ROWS[b[0][0]], WIDTH), jnp.float32) for b in names.values()],
        in_specs=[SMEM] * 4 + [VMEM] * 4 + [pl.BlockSpec(memory_space=pltpu.HBM)],
        out_specs=[VMEM] * len(names),
        scratch_shapes=[pltpu.VMEM((pieces[0].shape[0], TILE), jnp.bfloat16)] * 2
        + [pltpu.VMEM((8, TILE, WIDTH), jnp.float32), pltpu.SemaphoreType.DMA((8,))],
        **settings(cost),
    )(spots, *masks, *pieces, right)
    return dict(zip(names, outs))


def join(value, first, arrived, cost):
    def kernel(value_ref, arrived_ref, out_ref):
        del value_ref
        for n in range(arrived.shape[0]):
            out_ref[first + n] += arrived_ref[n]

    return pl.pallas_call(
        kernel,
        out_shape=jax.ShapeDtypeStruct(value.shape, value.dtype),
        in_specs=[VMEM] * 2,
        out_specs=VMEM,
        input_output_aliases={0: 0},
        **settings(cost),
    )(value, arrived)


def total(top, bottom):
    def kernel(*refs):
        out_ref = refs[-1]
        out_ref[: ROWS["A"]] = sum(ref[...] for ref in refs[1 : len(top)]) + refs[0][...]
        out_ref[ROWS["A"] :] = sum(ref[...] for ref in refs[len(top) + 1 : -1]) + refs[len(top)][...]

    return pl.pallas_call(
        kernel,
        out_shape=jax.ShapeDtypeStruct((TILE, WIDTH), jnp.float32),
        in_specs=[VMEM] * (len(top) + len(bottom)),
        **settings("last"),
    )(*top, *bottom)


def gather(value, here):
    between, beside, across = (permute(value, x=bits) for bits in (1, 3, 2))
    near = jnp.where(here, between, beside)
    far = jnp.where(here, value, across)
    return near, far


def both_cores(near, far):
    return near, far, permute(near, c=1), permute(far, c=1)


def shards(left, right, left_mask, right_mask, result_mask):
    yl, x, c, yh, z = (lax.axis_index(a) for a in AXES)
    spots = jnp.stack([yl, x, c, yh, z]).astype(jnp.int32)
    masks = (left_mask, right_mask, result_mask)
    here = x // 2 == yl
    rows_a = ROWS["A"]

    left_a, left_b = lax.optimization_barrier((left[:rows_a], left[rows_a:]))
    own = gather(left_a, here)
    other_row = permute(left, yl=1)
    rest = gather(lax.optimization_barrier(jnp.concatenate([left_b, other_row])), here)
    p = product(
        {0: (0, rows_a), 2: (0, rows_a)},
        {
            "via1": [("A", 2, 0), ("A", 2, 1)],
            "via3": [("A", 2, 2), ("A", 2, 3)],
            "own": [("A", 0, d) for d in range(4)],
        },
        spots,
        masks,
        both_cores(*own),
        right,
        "first",
    )
    from1 = along_y(p["via1"], 1)
    from3 = along_y(p["via3"], 3)
    rest, a_own = lax.optimization_barrier((rest, p["own"]))
    own_rows, other_rows = (0, ROWS["B"]), (ROWS["B"], ROWS["B"] + TILE)
    q = product(
        {1: other_rows, 3: other_rows, 0: own_rows, 2: own_rows},
        {
            "a1": [("A", 1, d) for d in range(4)],
            "a3": [("A", 3, d) for d in range(4)],
            "via1": [("B", 0, 2), ("B", 1, 2)],
            "via3": [("B", 2, 2), ("B", 3, 2)],
            "b1": [("B", d, 1) for d in range(4)],
            "b3": [("B", d, 3) for d in range(4)],
            "own": [("B", d, 0) for d in range(4)],
        },
        spots,
        masks,
        both_cores(*rest),
        right,
        "second",
    )
    top_parts = (
        along_y(join(q["a1"], 2, from3, "join_a"), 1),
        along_y(join(q["a3"], 0, from1, "join_a"), 3),
    )
    from1 = along_z(q["via1"], 1)
    from3 = along_z(q["via3"], 3)
    bottom_parts = (
        along_z(join(q["b1"], 2, from3, "join_b"), 1),
        along_z(join(q["b3"], 0, from1, "join_b"), 3),
    )
    a = [a_own[d] + top_parts[0][d] + top_parts[1][d] for d in range(4)]
    _, b_own = lax.optimization_barrier((a[2], q["own"]))
    b = [b_own[d] + bottom_parts[0][d] + bottom_parts[1][d] for d in range(4)]
    return total(
        [a[0], along_z(a[2], 2), along_z(a[1], 1), along_z(a[3], 3)],
        [b[0], along_y(b[2], 2), along_y(b[1], 1), along_y(b[3], 3)],
    )


def solution(mesh):
    torus = Mesh(mesh.devices.reshape(SIZES), AXES)
    in_specs = (
        P("yl", ("yh", "z", "x", "c")),
        P(("yh", "z", "yl"), ("x", "c")),
        P(),
        P(),
        P(),
    )
    return jax.shard_map(
        shards, mesh=torus, in_specs=in_specs, out_specs=P("yl", ("x", "c", "yh", "z")), check_vma=False
    )
```

```python
import jax
import jax.numpy as jnp
from jax import lax
from jax.experimental import pallas as pl
from jax.experimental.pallas import tpu as pltpu
from jax.sharding import Mesh
from jax.sharding import PartitionSpec as P

TILE = 512
WIDTH = 256
AXES = ("yl", "x", "c", "yh", "z")
SIZES = (2, 4, 2, 2, 4)
ROWS = {"A": 256, "B": 256}
COST = {"first": 1, "second": 1, "join_a": 1, "join_b": 1, "last": 1}
SMEM = pl.BlockSpec(memory_space=pltpu.SMEM)
VMEM = pl.BlockSpec(memory_space=pltpu.VMEM)


def permute(value, yl=0, x=0, c=0, yh=0, z=0):
    bits = (((yl * 4 + x) * 2 + c) * 2 + yh) * 4 + z
    return lax.ppermute(value, AXES, [(n, n ^ bits) for n in range(128)])


def along_y(value, bits):
    return permute(value, yl=bits % 2, yh=bits // 2)


def along_z(value, bits):
    return permute(value, z=bits)


def settings(cost):
    size = 48 if cost in ("first", "second") else 8
    return dict(
        compiler_params=pltpu.CompilerParams(vmem_limit_bytes=size * 2**20),
        cost_estimate=pl.CostEstimate(flops=1, bytes_accessed=COST[cost], transcendentals=0),
    )


def product_kernel(turns_all, plan, blocks, spots, left_mask, right_mask, result_mask, *rest):
    pieces, right, outs, (hi_ref, lo_ref, tiles, sems) = rest[:blocks], rest[blocks], rest[blocks + 1 : -4], rest[-4:]
    yl, x, c, yh, z = (spots[n] for n in range(5))
    k = (yh * 4 + z) * 2 + yl
    first = (x * 2 + c) * 4
    near = 1 - lax.rem(x, 2)

    def used(dy, chunk):
        i = lax.rem(yl + dy % 2, 2)
        j = first + lax.div(chunk, 2)
        return left_mask[i, k] * right_mask[k, j] * result_mask[i, j] > 0

    def fetch(n, chunk):
        where = pl.ds(pl.multiple_of(chunk * WIDTH, WIDTH), WIDTH)
        return pltpu.make_async_copy(right.at[:, where], tiles.at[n], sems.at[n])

    groups = [
        (n, lax.rem(yh + high, 2) * 4 + jnp.bitwise_xor(z, dz), [dy for dy in turns_all if dy // 2 == high], dz)
        for n, (high, dz) in enumerate((high, dz) for high in range(2) for dz in range(4))
    ]

    def wanted(chunk, turns):
        flag = used(turns[0], chunk)
        for dy in turns[1:]:
            flag = jnp.logical_or(flag, used(dy, chunk))
        return flag

    for n, chunk, turns, _ in groups:

        @pl.when(wanted(chunk, turns))
        def _():
            fetch(n, chunk).start()

    if blocks == 2:
        cores = [(c, pieces[0]), (1 - c, pieces[1])]
    else:
        cores = [(core, pieces[0].at[core]) for core in range(2)]
    for core, piece in cores:
        for n, chip in enumerate((near, 1 - near)):
            value = piece[n]
            hi = value.astype(jnp.bfloat16)
            where = pl.ds(pl.multiple_of(chip * 256 + core * 128, 128), 128)
            hi_ref[:, where] = hi
            lo_ref[:, where] = (value - hi.astype(jnp.float32)).astype(jnp.bfloat16)
    for n, chunk, turns, dz in groups:

        @pl.when(wanted(chunk, turns))
        def _():
            fetch(n, chunk).wait()

        for dy in turns:

            @pl.when(used(dy, chunk))
            def _():
                tile = tiles[n]
                hi = tile.astype(jnp.bfloat16)
                lo = (tile - hi.astype(jnp.float32)).astype(jnp.bfloat16)
                total = jnp.dot(hi_ref[...], hi, preferred_element_type=jnp.float32)
                total += jnp.dot(hi_ref[...], lo, preferred_element_type=jnp.float32)
                total += jnp.dot(lo_ref[...], hi, preferred_element_type=jnp.float32)
                done = 0
                for half, out, slot in plan[dy, dz]:
                    outs[out][slot] = total[done : done + ROWS[half]]
                    done += ROWS[half]

            @pl.when(jnp.logical_not(used(dy, chunk)))
            def _():
                for half, out, slot in plan[dy, dz]:
                    outs[out][slot] = jnp.zeros((ROWS[half], WIDTH), jnp.float32)


def product(turns, names, spots, masks, pieces, right, cost):
    plan = {
        (dy, dz): [
            (half, n, blocks.index((half, dy, dz)))
            for half in "AB"
            for n, blocks in enumerate(names.values())
            if (half, dy, dz) in blocks
        ]
        for dy in turns
        for dz in range(4)
    }
    outs = pl.pallas_call(
        lambda *refs: product_kernel(turns, plan, len(pieces), *refs),
        out_shape=[jax.ShapeDtypeStruct((len(b), ROWS[b[0][0]], WIDTH), jnp.float32) for b in names.values()],
        in_specs=[SMEM] * 4 + [VMEM] * len(pieces) + [pl.BlockSpec(memory_space=pltpu.HBM)],
        out_specs=[VMEM] * len(names),
        scratch_shapes=[pltpu.VMEM((TILE, TILE), jnp.bfloat16)] * 2
        + [pltpu.VMEM((8, TILE, WIDTH), jnp.float32), pltpu.SemaphoreType.DMA((8,))],
        **settings(cost),
    )(spots, *masks, *pieces, right)
    return dict(zip(names, outs))


def join(value, first, arrived, cost, kept=None):
    def kernel(value_ref, arrived_ref, *rest):
        out_ref = rest[-1]
        del value_ref
        for n in range(count):
            out_ref[first + n] = (rest[0][n] if kept is not None else out_ref[first + n]) + arrived_ref[n]

    count = min(value.shape[0] - first, arrived.shape[0])
    operands = [value, arrived] + ([] if kept is None else [kept])
    return pl.pallas_call(
        kernel,
        out_shape=jax.ShapeDtypeStruct(value.shape, value.dtype),
        in_specs=[VMEM] * len(operands),
        out_specs=VMEM,
        input_output_aliases={0: 0},
        **settings(cost),
    )(*operands)


def total(top, bottom):
    def kernel(*refs):
        out_ref = refs[-1]
        out_ref[: ROWS["A"]] = sum(ref[...] for ref in refs[1 : len(top)]) + refs[0][...]
        out_ref[ROWS["A"] :] = sum(ref[...] for ref in refs[len(top) + 1 : -1]) + refs[len(top)][...]

    return pl.pallas_call(
        kernel,
        out_shape=jax.ShapeDtypeStruct((TILE, WIDTH), jnp.float32),
        in_specs=[VMEM] * (len(top) + len(bottom)),
        **settings("last"),
    )(*top, *bottom)


def both_cores(value):
    return lax.all_to_all(jnp.broadcast_to(value[None], (2, *value.shape)), "c", 0, 0, tiled=True)


def shards(left, right, left_mask, right_mask, result_mask):
    yl, x, c, yh, z = (lax.axis_index(a) for a in AXES)
    spots = jnp.stack([yl, x, c, yh, z]).astype(jnp.int32)
    masks = (left_mask, right_mask, result_mask)

    here = x // 2 == yl
    across, beside, between = (permute(left, x=bits) for bits in (2, 3, 1))
    mine = jnp.stack([jnp.where(here, between, beside), jnp.where(here, left, across)])
    others = jnp.stack([jnp.where(here, beside, between), jnp.where(here, across, left)])
    others = along_y(others, 1)
    p = product(
        (0, 2),
        {
            "y1": [("A", 2, 0), ("A", 2, 1)],
            "y3": [("A", 2, 2), ("A", 2, 3)],
            "z1": [("B", 0, 2), ("B", 0, 1)],
            "z3": [("B", 2, 2), ("B", 2, 3)],
            "z1_kept": [("B", 2, 1)],
            "z3_kept": [("B", 0, 3)],
            "a": [("A", 0, d) for d in range(4)],
            "b": [("B", 0, 0), ("B", 2, 0)],
        },
        spots,
        masks,
        (mine, permute(mine, c=1)),
        right,
        "first",
    )
    from_y1 = along_y(p["y1"], 1)
    from_y3 = along_y(p["y3"], 3)
    from_z1 = along_z(p["z1"], 1)
    from_z3 = along_z(p["z3"], 3)
    others, a_own = lax.optimization_barrier((others, p["a"]))
    q = product(
        (1, 3),
        {
            "y1": [("A", 1, d) for d in range(4)],
            "y3": [("A", 3, d) for d in range(4)],
            "z1": [("B", 1, 2), ("B", 1, 1), ("B", 1, 1)],
            "z3": [("B", 3, 2), ("B", 3, 3), ("B", 3, 3)],
            "z1_last": [("B", 3, 1)],
            "z3_last": [("B", 1, 3)],
            "b": [("B", 1, 0), ("B", 3, 0)],
        },
        spots,
        masks,
        (both_cores(others),),
        right,
        "second",
    )
    sum_y1 = along_y(join(q["y1"], 2, from_y3, "join_a"), 1)
    sum_y3 = along_y(join(q["y3"], 0, from_y1, "join_a"), 3)
    next_z1 = along_z(join(q["z1"], 2, from_z3, "join_b", p["z1_kept"]), 1)
    next_z3 = along_z(join(q["z3"], 2, from_z1, "join_b", p["z3_kept"]), 3)
    last_z1 = along_z(join(q["z1_last"], 0, next_z3, "join_b"), 1)
    last_z3 = along_z(join(q["z3_last"], 0, next_z1, "join_b"), 3)
    a = [a_own[d] + sum_y1[d] + sum_y3[d] for d in range(4)]
    b = [
        p["b"][0] + from_z1[1] + next_z3[2],
        q["b"][0] + next_z1[1] + last_z3[0],
        p["b"][1] + next_z1[2] + from_z3[1],
        q["b"][1] + last_z1[0] + next_z3[1],
    ]
    return total(
        [a[0], along_z(a[2], 2), along_z(a[1], 1), along_z(a[3], 3)],
        [b[0], along_y(b[2], 2), along_y(b[1], 1), along_y(b[3], 3)],
    )


def solution(mesh):
    torus = Mesh(mesh.devices.reshape(SIZES), AXES)
    in_specs = (
        P("yl", ("yh", "z", "x", "c")),
        P(("yh", "z", "yl"), ("x", "c")),
        P(),
        P(),
        P(),
    )
    return jax.shard_map(
        shards, mesh=torus, in_specs=in_specs, out_specs=P("yl", ("x", "c", "yh", "z")), check_vma=False
    )
```

```python
import jax
import jax.numpy as jnp
from jax import lax
from jax.experimental import pallas as pl
from jax.experimental.pallas import tpu as pltpu
from jax.sharding import Mesh
from jax.sharding import PartitionSpec as P

TILE = 512
WIDTH = 256
AXES = ("yl", "x", "c", "yh", "z")
SIZES = (2, 4, 2, 2, 4)
ROWS = {"A": 256, "B": 256}
COST = {"first": 1, "second": 1, "join_a": 1, "join_b": 1, "last": 1}
SMEM = pl.BlockSpec(memory_space=pltpu.SMEM)
VMEM = pl.BlockSpec(memory_space=pltpu.VMEM)


def permute(value, yl=0, x=0, c=0, yh=0, z=0):
    bits = (((yl * 4 + x) * 2 + c) * 2 + yh) * 4 + z
    return lax.ppermute(value, AXES, [(n, n ^ bits) for n in range(128)])


def along_y(value, bits):
    return permute(value, yl=bits % 2, yh=bits // 2)


def along_z(value, bits):
    return permute(value, z=bits)


def settings(cost):
    size = 48 if cost in ("first", "second") else 8
    return dict(
        compiler_params=pltpu.CompilerParams(vmem_limit_bytes=size * 2**20),
        cost_estimate=pl.CostEstimate(flops=1, bytes_accessed=COST[cost], transcendentals=0),
    )


def product_kernel(turns_all, plan, blocks, spots, left_mask, right_mask, result_mask, *rest):
    pieces, right, outs, (hi_ref, lo_ref, tiles, sems) = rest[:blocks], rest[blocks], rest[blocks + 1 : -4], rest[-4:]
    yl, x, c, yh, z = (spots[n] for n in range(5))
    k = (yh * 4 + z) * 2 + yl
    first = (x * 2 + c) * 4
    near = 1 - lax.rem(x, 2)

    def used(dy, chunk):
        i = lax.rem(yl + dy % 2, 2)
        j = first + lax.div(chunk, 2)
        return left_mask[i, k] * right_mask[k, j] * result_mask[i, j] > 0

    def fetch(n, chunk):
        where = pl.ds(pl.multiple_of(chunk * WIDTH, WIDTH), WIDTH)
        return pltpu.make_async_copy(right.at[:, where], tiles.at[n], sems.at[n])

    groups = [
        (n, lax.rem(yh + high, 2) * 4 + jnp.bitwise_xor(z, dz), [dy for dy in turns_all if dy // 2 == high], dz)
        for n, (high, dz) in enumerate((high, dz) for high in range(2) for dz in range(4))
    ]

    def wanted(chunk, turns):
        flag = used(turns[0], chunk)
        for dy in turns[1:]:
            flag = jnp.logical_or(flag, used(dy, chunk))
        return flag

    for n, chunk, turns, _ in groups:

        @pl.when(wanted(chunk, turns))
        def _():
            fetch(n, chunk).start()

    if blocks == 2:
        cores = [(c, pieces[0]), (1 - c, pieces[1])]
    else:
        cores = [(core, pieces[0].at[core]) for core in range(2)]
    for core, piece in cores:
        for n, chip in enumerate((near, 1 - near)):
            value = piece[n]
            hi = value.astype(jnp.bfloat16)
            where = pl.ds(pl.multiple_of(chip * 256 + core * 128, 128), 128)
            hi_ref[:, where] = hi
            lo_ref[:, where] = (value - hi.astype(jnp.float32)).astype(jnp.bfloat16)
    for n, chunk, turns, dz in groups:

        @pl.when(wanted(chunk, turns))
        def _():
            fetch(n, chunk).wait()

        for dy in turns:

            @pl.when(used(dy, chunk))
            def _():
                tile = tiles[n]
                hi = tile.astype(jnp.bfloat16)
                lo = (tile - hi.astype(jnp.float32)).astype(jnp.bfloat16)
                total = jnp.dot(hi_ref[...], hi, preferred_element_type=jnp.float32)
                total += jnp.dot(hi_ref[...], lo, preferred_element_type=jnp.float32)
                total += jnp.dot(lo_ref[...], hi, preferred_element_type=jnp.float32)
                done = 0
                for half, out, slot in plan[dy, dz]:
                    outs[out][slot] = total[done : done + ROWS[half]]
                    done += ROWS[half]

            @pl.when(jnp.logical_not(used(dy, chunk)))
            def _():
                for half, out, slot in plan[dy, dz]:
                    outs[out][slot] = jnp.zeros((ROWS[half], WIDTH), jnp.float32)


def product(turns, names, spots, masks, pieces, right, cost):
    plan = {
        (dy, dz): [
            (half, n, blocks.index((half, dy, dz)))
            for half in "AB"
            for n, blocks in enumerate(names.values())
            if (half, dy, dz) in blocks
        ]
        for dy in turns
        for dz in range(4)
    }
    outs = pl.pallas_call(
        lambda *refs: product_kernel(turns, plan, len(pieces), *refs),
        out_shape=[jax.ShapeDtypeStruct((len(b), ROWS[b[0][0]], WIDTH), jnp.float32) for b in names.values()],
        in_specs=[SMEM] * 4 + [VMEM] * len(pieces) + [pl.BlockSpec(memory_space=pltpu.HBM)],
        out_specs=[VMEM] * len(names),
        scratch_shapes=[pltpu.VMEM((TILE, TILE), jnp.bfloat16)] * 2
        + [pltpu.VMEM((8, TILE, WIDTH), jnp.float32), pltpu.SemaphoreType.DMA((8,))],
        **settings(cost),
    )(spots, *masks, *pieces, right)
    return dict(zip(names, outs))


def join(value, first, arrived, cost, kept=None):
    def kernel(value_ref, arrived_ref, *rest):
        out_ref = rest[-1]
        del value_ref
        for n in range(count):
            out_ref[first + n] = (rest[0][n] if kept is not None else out_ref[first + n]) + arrived_ref[n]

    count = min(value.shape[0] - first, arrived.shape[0])
    operands = [value, arrived] + ([] if kept is None else [kept])
    return pl.pallas_call(
        kernel,
        out_shape=jax.ShapeDtypeStruct(value.shape, value.dtype),
        in_specs=[VMEM] * len(operands),
        out_specs=VMEM,
        input_output_aliases={0: 0},
        **settings(cost),
    )(*operands)


def total(top, bottom):
    def kernel(*refs):
        out_ref = refs[-1]
        out_ref[: ROWS["A"]] = sum(ref[...] for ref in refs[1 : len(top)]) + refs[0][...]
        out_ref[ROWS["A"] :] = sum(ref[...] for ref in refs[len(top) + 1 : -1]) + refs[len(top)][...]

    return pl.pallas_call(
        kernel,
        out_shape=jax.ShapeDtypeStruct((TILE, WIDTH), jnp.float32),
        in_specs=[VMEM] * (len(top) + len(bottom)),
        **settings("last"),
    )(*top, *bottom)


def both_cores(value):
    return lax.all_to_all(jnp.broadcast_to(value[None], (2, *value.shape)), "c", 0, 0, tiled=True)


def shards(left, right, left_mask, right_mask, result_mask):
    yl, x, c, yh, z = (lax.axis_index(a) for a in AXES)
    spots = jnp.stack([yl, x, c, yh, z]).astype(jnp.int32)
    masks = (left_mask, right_mask, result_mask)

    here = x // 2 == yl
    across, beside, between = (permute(left, x=bits) for bits in (2, 3, 1))
    mine = jnp.stack([jnp.where(here, between, beside), jnp.where(here, left, across)])
    others = jnp.stack([jnp.where(here, beside, between), jnp.where(here, across, left)])
    others = along_y(others, 1)
    p = product(
        (0, 2),
        {
            "y1": [("A", 2, 0)],
            "y3": [("A", 2, 1), ("A", 2, 2), ("A", 2, 3)],
            "z1": [("B", 0, 2), ("B", 0, 1)],
            "z3": [("B", 2, 2), ("B", 2, 3)],
            "z1_kept": [("B", 2, 1)],
            "z3_kept": [("B", 0, 3)],
            "a": [("A", 0, d) for d in range(4)],
            "b": [("B", 0, 0), ("B", 2, 0)],
        },
        spots,
        masks,
        (mine, permute(mine, c=1)),
        right,
        "first",
    )
    from_y1 = along_y(p["y1"], 1)
    from_y3 = along_y(p["y3"], 3)
    from_z1 = along_z(p["z1"], 1)
    from_z3 = along_z(p["z3"], 3)
    others, a_own = lax.optimization_barrier((others, p["a"]))
    others, from_y1 = lax.optimization_barrier((both_cores(others), from_y1))
    q = product(
        (1, 3),
        {
            "y1": [("A", 1, d) for d in range(4)],
            "y3": [("A", 3, d) for d in range(4)],
            "z1": [("B", 1, 2), ("B", 1, 1), ("B", 1, 1)],
            "z3": [("B", 3, 2), ("B", 3, 3), ("B", 3, 3)],
            "z1_last": [("B", 3, 1)],
            "z3_last": [("B", 1, 3)],
            "b": [("B", 1, 0), ("B", 3, 0)],
        },
        spots,
        masks,
        (others,),
        right,
        "second",
    )
    sum_y1 = along_y(join(q["y1"], 1, from_y3, "join_a"), 1)
    sum_y3 = along_y(join(q["y3"], 0, from_y1, "join_a"), 3)
    next_z1 = along_z(join(q["z1"], 2, from_z3, "join_b", p["z1_kept"]), 1)
    next_z3 = along_z(join(q["z3"], 2, from_z1, "join_b", p["z3_kept"]), 3)
    last_z1 = along_z(join(q["z1_last"], 0, next_z3, "join_b"), 1)
    last_z3 = along_z(join(q["z3_last"], 0, next_z1, "join_b"), 3)
    a = [a_own[d] + sum_y1[d] + sum_y3[d] for d in range(4)]
    b = [
        p["b"][0] + from_z1[1] + next_z3[2],
        q["b"][0] + next_z1[1] + last_z3[0],
        p["b"][1] + next_z1[2] + from_z3[1],
        q["b"][1] + last_z1[0] + next_z3[1],
    ]
    return total(
        [a[0], along_z(a[1], 1), along_z(a[3], 3), along_z(a[2], 2)],
        [b[0], along_y(b[2], 2), along_y(b[1], 1), along_y(b[3], 3)],
    )


def solution(mesh):
    torus = Mesh(mesh.devices.reshape(SIZES), AXES)
    in_specs = (
        P("yl", ("yh", "z", "x", "c")),
        P(("yh", "z", "yl"), ("x", "c")),
        P(),
        P(),
        P(),
    )
    return jax.shard_map(
        shards, mesh=torus, in_specs=in_specs, out_specs=P("yl", ("x", "c", "yh", "z")), check_vma=False
    )
```

```python
import jax
import jax.numpy as jnp
from jax import lax
from jax.experimental import pallas as pl
from jax.experimental.pallas import tpu as pltpu
from jax.sharding import Mesh
from jax.sharding import PartitionSpec as P

TILE = 512
WIDTH = 256
AXES = ("yl", "x", "c", "yh", "z")
SIZES = (2, 4, 2, 2, 4)
ROWS = {"A": 256, "B": 256}
COST = {"split": 1, "first": 1, "second": 1, "join_a": 1, "join_b": 1, "last": 1}
SMEM = pl.BlockSpec(memory_space=pltpu.SMEM)
VMEM = pl.BlockSpec(memory_space=pltpu.VMEM)


def permute(value, yl=0, x=0, c=0, yh=0, z=0):
    bits = (((yl * 4 + x) * 2 + c) * 2 + yh) * 4 + z
    return lax.ppermute(value, AXES, [(n, n ^ bits) for n in range(128)])


def along_y(value, bits):
    return permute(value, yl=bits % 2, yh=bits // 2)


def along_z(value, bits):
    return permute(value, z=bits)


def settings(cost):
    size = 48 if cost == "split" else 8
    return dict(
        compiler_params=pltpu.CompilerParams(vmem_limit_bytes=size * 2**20),
        cost_estimate=pl.CostEstimate(flops=1, bytes_accessed=COST[cost], transcendentals=0),
    )


def split_kernel(spots, left_mask, right_mask, result_mask, right, hi_ref, lo_ref, tiles, sems):
    yl, x, c, yh, z = (spots[n] for n in range(5))
    k = (yh * 4 + z) * 2 + yl
    first = (x * 2 + c) * 4

    def block(n):
        chunk = lax.rem(yh + n // 4, 2) * 4 + jnp.bitwise_xor(z, n % 4)
        j = first + lax.div(chunk, 2)
        used = right_mask[k, j] * (left_mask[0, k] * result_mask[0, j] + left_mask[1, k] * result_mask[1, j]) > 0
        where = pl.ds(pl.multiple_of(chunk * WIDTH, WIDTH), WIDTH)
        return used, pltpu.make_async_copy(right.at[:, where], tiles.at[n], sems.at[n])

    for n in range(8):
        used, copy = block(n)

        @pl.when(used)
        def _():
            copy.start()

    for n in range(8):
        used, copy = block(n)

        @pl.when(used)
        def _():
            copy.wait()
            tile = tiles[n]
            hi = tile.astype(jnp.bfloat16)
            hi_ref[n] = hi
            lo_ref[n] = (tile - hi.astype(jnp.float32)).astype(jnp.bfloat16)


def split(spots, masks, right):
    return pl.pallas_call(
        split_kernel,
        out_shape=[jax.ShapeDtypeStruct((8, TILE, WIDTH), jnp.bfloat16)] * 2,
        in_specs=[SMEM] * 4 + [pl.BlockSpec(memory_space=pltpu.HBM)],
        out_specs=[VMEM] * 2,
        scratch_shapes=[pltpu.VMEM((8, TILE, WIDTH), jnp.float32), pltpu.SemaphoreType.DMA((8,))],
        **settings("split"),
    )(spots, *masks, right)


def product_kernel(turns_all, plan, blocks, spots, left_mask, right_mask, result_mask, *rest):
    pieces, right, outs, (hi_ref, lo_ref) = rest[:blocks], rest[blocks : blocks + 2], rest[blocks + 2 : -2], rest[-2:]
    yl, x, c, yh, z = (spots[n] for n in range(5))
    k = (yh * 4 + z) * 2 + yl
    first = (x * 2 + c) * 4
    near = 1 - lax.rem(x, 2)

    def used(dy, chunk):
        i = lax.rem(yl + dy % 2, 2)
        j = first + lax.div(chunk, 2)
        return left_mask[i, k] * right_mask[k, j] * result_mask[i, j] > 0

    groups = [
        (n, lax.rem(yh + high, 2) * 4 + jnp.bitwise_xor(z, dz), [dy for dy in turns_all if dy // 2 == high], dz)
        for n, (high, dz) in enumerate((high, dz) for high in range(2) for dz in range(4))
    ]

    if blocks == 2:
        cores = [(c, pieces[0]), (1 - c, pieces[1])]
    else:
        cores = [(core, pieces[0].at[core]) for core in range(2)]
    for core, piece in cores:
        for n, chip in enumerate((near, 1 - near)):
            value = piece[n]
            hi = value.astype(jnp.bfloat16)
            where = pl.ds(pl.multiple_of(chip * 256 + core * 128, 128), 128)
            hi_ref[:, where] = hi
            lo_ref[:, where] = (value - hi.astype(jnp.float32)).astype(jnp.bfloat16)
    for n, chunk, turns, dz in groups:

        for dy in turns:

            @pl.when(used(dy, chunk))
            def _():
                hi, lo = right[0][n], right[1][n]
                total = jnp.dot(hi_ref[...], hi, preferred_element_type=jnp.float32)
                total += jnp.dot(hi_ref[...], lo, preferred_element_type=jnp.float32)
                total += jnp.dot(lo_ref[...], hi, preferred_element_type=jnp.float32)
                done = 0
                for half, out, slot in plan[dy, dz]:
                    outs[out][slot] = total[done : done + ROWS[half]]
                    done += ROWS[half]

            @pl.when(jnp.logical_not(used(dy, chunk)))
            def _():
                for half, out, slot in plan[dy, dz]:
                    outs[out][slot] = jnp.zeros((ROWS[half], WIDTH), jnp.float32)


def product(turns, names, spots, masks, pieces, right, cost):
    plan = {
        (dy, dz): [
            (half, n, blocks.index((half, dy, dz)))
            for half in "AB"
            for n, blocks in enumerate(names.values())
            if (half, dy, dz) in blocks
        ]
        for dy in turns
        for dz in range(4)
    }
    outs = pl.pallas_call(
        lambda *refs: product_kernel(turns, plan, len(pieces), *refs),
        out_shape=[jax.ShapeDtypeStruct((len(b), ROWS[b[0][0]], WIDTH), jnp.float32) for b in names.values()],
        in_specs=[SMEM] * 4 + [VMEM] * (len(pieces) + 2),
        out_specs=[VMEM] * len(names),
        scratch_shapes=[pltpu.VMEM((TILE, TILE), jnp.bfloat16)] * 2,
        **settings(cost),
    )(spots, *masks, *pieces, *right)
    return dict(zip(names, outs))


def join(value, first, arrived, cost, kept=None):
    def kernel(value_ref, arrived_ref, *rest):
        out_ref = rest[-1]
        del value_ref
        for n in range(count):
            out_ref[first + n] = (rest[0][n] if kept is not None else out_ref[first + n]) + arrived_ref[n]

    count = min(value.shape[0] - first, arrived.shape[0])
    operands = [value, arrived] + ([] if kept is None else [kept])
    return pl.pallas_call(
        kernel,
        out_shape=jax.ShapeDtypeStruct(value.shape, value.dtype),
        in_specs=[VMEM] * len(operands),
        out_specs=VMEM,
        input_output_aliases={0: 0},
        **settings(cost),
    )(*operands)


def total(top, bottom):
    def kernel(*refs):
        out_ref = refs[-1]
        out_ref[: ROWS["A"]] = sum(ref[...] for ref in refs[1 : len(top)]) + refs[0][...]
        out_ref[ROWS["A"] :] = sum(ref[...] for ref in refs[len(top) + 1 : -1]) + refs[len(top)][...]

    return pl.pallas_call(
        kernel,
        out_shape=jax.ShapeDtypeStruct((TILE, WIDTH), jnp.float32),
        in_specs=[VMEM] * (len(top) + len(bottom)),
        **settings("last"),
    )(*top, *bottom)


def both_cores(value):
    return lax.all_to_all(jnp.broadcast_to(value[None], (2, *value.shape)), "c", 0, 0, tiled=True)


def shards(left, right, left_mask, right_mask, result_mask):
    yl, x, c, yh, z = (lax.axis_index(a) for a in AXES)
    spots = jnp.stack([yl, x, c, yh, z]).astype(jnp.int32)
    masks = (left_mask, right_mask, result_mask)

    here = x // 2 == yl
    across, beside, between = (permute(left, x=bits) for bits in (2, 3, 1))
    right = split(spots, masks, right)
    across, right = lax.optimization_barrier((across, right))
    mine = jnp.stack([jnp.where(here, between, beside), jnp.where(here, left, across)])
    others = jnp.stack([jnp.where(here, beside, between), jnp.where(here, across, left)])
    others = along_y(others, 1)
    p = product(
        (0, 2),
        {
            "y1": [("A", 2, 0)],
            "y3": [("A", 2, 1), ("A", 2, 2), ("A", 2, 3)],
            "z1": [("B", 0, 2), ("B", 0, 1)],
            "z3": [("B", 2, 2), ("B", 2, 3)],
            "z1_kept": [("B", 2, 1)],
            "z3_kept": [("B", 0, 3)],
            "a": [("A", 0, d) for d in range(4)],
            "b": [("B", 0, 0), ("B", 2, 0)],
        },
        spots,
        masks,
        (mine, permute(mine, c=1)),
        right,
        "first",
    )
    from_y1 = along_y(p["y1"], 1)
    from_y3 = along_y(p["y3"], 3)
    from_z1 = along_z(p["z1"], 1)
    from_z3 = along_z(p["z3"], 3)
    others, a_own = lax.optimization_barrier((others, p["a"]))
    others, from_y1 = lax.optimization_barrier((both_cores(others), from_y1))
    q = product(
        (1, 3),
        {
            "y1": [("A", 1, d) for d in range(4)],
            "y3": [("A", 3, d) for d in range(4)],
            "z1": [("B", 1, 2), ("B", 1, 1), ("B", 1, 1)],
            "z3": [("B", 3, 2), ("B", 3, 3), ("B", 3, 3)],
            "z1_last": [("B", 3, 1)],
            "z3_last": [("B", 1, 3)],
            "b": [("B", 1, 0), ("B", 3, 0)],
        },
        spots,
        masks,
        (others,),
        right,
        "second",
    )
    sum_y1 = along_y(join(q["y1"], 1, from_y3, "join_a"), 1)
    sum_y3 = along_y(join(q["y3"], 0, from_y1, "join_a"), 3)
    next_z1 = along_z(join(q["z1"], 2, from_z3, "join_b", p["z1_kept"]), 1)
    next_z3 = along_z(join(q["z3"], 2, from_z1, "join_b", p["z3_kept"]), 3)
    last_z1 = along_z(join(q["z1_last"], 0, next_z3, "join_b"), 1)
    last_z3 = along_z(join(q["z3_last"], 0, next_z1, "join_b"), 3)
    a = [a_own[d] + sum_y1[d] + sum_y3[d] for d in range(4)]
    b = [
        p["b"][0] + from_z1[1] + next_z3[2],
        q["b"][0] + next_z1[1] + last_z3[0],
        p["b"][1] + next_z1[2] + from_z3[1],
        q["b"][1] + last_z1[0] + next_z3[1],
    ]
    return total(
        [a[0], along_z(a[1], 1), along_z(a[3], 3), along_z(a[2], 2)],
        [b[0], along_y(b[2], 2), along_y(b[1], 1), along_y(b[3], 3)],
    )


def solution(mesh):
    torus = Mesh(mesh.devices.reshape(SIZES), AXES)
    in_specs = (
        P("yl", ("yh", "z", "x", "c")),
        P(("yh", "z", "yl"), ("x", "c")),
        P(),
        P(),
        P(),
    )
    return jax.shard_map(
        shards, mesh=torus, in_specs=in_specs, out_specs=P("yl", ("x", "c", "yh", "z")), check_vma=False
    )
```

```python
import jax
import jax.numpy as jnp
from jax import lax
from jax.experimental import pallas as pl
from jax.experimental.pallas import tpu as pltpu
from jax.sharding import Mesh
from jax.sharding import PartitionSpec as P

TILE = 512
WIDTH = 256
AXES = ("yl", "x", "c", "yh", "z")
SIZES = (2, 4, 2, 2, 4)
ROWS = {"A": 256, "B": 256}
COST = {"split": 1, "first": 1, "second": 1, "join_a": 1, "join_b": 1, "last": 1}
SMEM = pl.BlockSpec(memory_space=pltpu.SMEM)
VMEM = pl.BlockSpec(memory_space=pltpu.VMEM)


def permute(value, yl=0, x=0, c=0, yh=0, z=0):
    bits = (((yl * 4 + x) * 2 + c) * 2 + yh) * 4 + z
    return lax.ppermute(value, AXES, [(n, n ^ bits) for n in range(128)])


def along_y(value, bits):
    return permute(value, yl=bits % 2, yh=bits // 2)


def along_z(value, bits):
    return permute(value, z=bits)


def settings(cost):
    size = 48 if cost == "split" else 8
    return dict(
        compiler_params=pltpu.CompilerParams(vmem_limit_bytes=size * 2**20),
        cost_estimate=pl.CostEstimate(flops=1, bytes_accessed=COST[cost], transcendentals=0),
    )


def split_kernel(spots, left_mask, right_mask, result_mask, right, hi_ref, lo_ref, tiles, sems):
    yl, x, c, yh, z = (spots[n] for n in range(5))
    k = (yh * 4 + z) * 2 + yl
    first = (x * 2 + c) * 4

    def block(n):
        chunk = lax.rem(yh + n // 4, 2) * 4 + jnp.bitwise_xor(z, n % 4)
        j = first + lax.div(chunk, 2)
        used = right_mask[k, j] * (left_mask[0, k] * result_mask[0, j] + left_mask[1, k] * result_mask[1, j]) > 0
        where = pl.ds(pl.multiple_of(chunk * WIDTH, WIDTH), WIDTH)
        return used, pltpu.make_async_copy(right.at[:, where], tiles.at[n], sems.at[n])

    for n in range(8):
        used, copy = block(n)

        @pl.when(used)
        def _():
            copy.start()

    for n in range(8):
        used, copy = block(n)

        @pl.when(used)
        def _():
            copy.wait()
            tile = tiles[n]
            hi = tile.astype(jnp.bfloat16)
            hi_ref[n] = hi
            lo_ref[n] = (tile - hi.astype(jnp.float32)).astype(jnp.bfloat16)


def split(spots, masks, right):
    return pl.pallas_call(
        split_kernel,
        out_shape=[jax.ShapeDtypeStruct((8, TILE, WIDTH), jnp.bfloat16)] * 2,
        in_specs=[SMEM] * 4 + [pl.BlockSpec(memory_space=pltpu.HBM)],
        out_specs=[VMEM] * 2,
        scratch_shapes=[pltpu.VMEM((8, TILE, WIDTH), jnp.float32), pltpu.SemaphoreType.DMA((8,))],
        **settings("split"),
    )(spots, *masks, right)


def product_kernel(turns_all, plan, blocks, spots, left_mask, right_mask, result_mask, *rest):
    pieces, right, outs, (hi_ref, lo_ref) = rest[:blocks], rest[blocks : blocks + 2], rest[blocks + 2 : -2], rest[-2:]
    yl, x, c, yh, z = (spots[n] for n in range(5))
    k = (yh * 4 + z) * 2 + yl
    first = (x * 2 + c) * 4
    near = 1 - lax.rem(x, 2)

    def used(dy, chunk):
        i = lax.rem(yl + dy % 2, 2)
        j = first + lax.div(chunk, 2)
        return left_mask[i, k] * right_mask[k, j] * result_mask[i, j] > 0

    groups = [
        (n, lax.rem(yh + high, 2) * 4 + jnp.bitwise_xor(z, dz), [dy for dy in turns_all if dy // 2 == high], dz)
        for n, (high, dz) in enumerate((high, dz) for high in range(2) for dz in range(4))
    ]

    if blocks == 2:
        cores = [(c, pieces[0]), (1 - c, pieces[1])]
    else:
        cores = [(core, pieces[0].at[core]) for core in range(2)]
    for core, piece in cores:
        for n, chip in enumerate((near, 1 - near)):
            value = piece[n]
            hi = value.astype(jnp.bfloat16)
            where = pl.ds(pl.multiple_of(chip * 256 + core * 128, 128), 128)
            hi_ref[:, where] = hi
            lo_ref[:, where] = (value - hi.astype(jnp.float32)).astype(jnp.bfloat16)
    for n, chunk, turns, dz in groups:

        for dy in turns:

            @pl.when(used(dy, chunk))
            def _():
                hi, lo = right[0][n], right[1][n]
                total = jnp.dot(hi_ref[...], hi, preferred_element_type=jnp.float32)
                total += jnp.dot(hi_ref[...], lo, preferred_element_type=jnp.float32)
                total += jnp.dot(lo_ref[...], hi, preferred_element_type=jnp.float32)
                done = 0
                for half, out, slot in plan[dy, dz]:
                    outs[out][slot] = total[done : done + ROWS[half]]
                    done += ROWS[half]

            @pl.when(jnp.logical_not(used(dy, chunk)))
            def _():
                for half, out, slot in plan[dy, dz]:
                    outs[out][slot] = jnp.zeros((ROWS[half], WIDTH), jnp.float32)


def product(turns, names, spots, masks, pieces, right, cost):
    plan = {
        (dy, dz): [
            (half, n, blocks.index((half, dy, dz)))
            for half in "AB"
            for n, blocks in enumerate(names.values())
            if (half, dy, dz) in blocks
        ]
        for dy in turns
        for dz in range(4)
    }
    outs = pl.pallas_call(
        lambda *refs: product_kernel(turns, plan, len(pieces), *refs),
        out_shape=[jax.ShapeDtypeStruct((len(b), ROWS[b[0][0]], WIDTH), jnp.float32) for b in names.values()],
        in_specs=[SMEM] * 4 + [VMEM] * (len(pieces) + 2),
        out_specs=[VMEM] * len(names),
        scratch_shapes=[pltpu.VMEM((TILE, TILE), jnp.bfloat16)] * 2,
        **settings(cost),
    )(spots, *masks, *pieces, *right)
    return dict(zip(names, outs))


def join(value, first, arrived, cost, kept=None):
    def kernel(value_ref, arrived_ref, *rest):
        out_ref = rest[-1]
        del value_ref
        for n in range(count):
            out_ref[first + n] = (rest[0][n] if kept is not None else out_ref[first + n]) + arrived_ref[n]

    count = min(value.shape[0] - first, arrived.shape[0])
    operands = [value, arrived] + ([] if kept is None else [kept])
    return pl.pallas_call(
        kernel,
        out_shape=jax.ShapeDtypeStruct(value.shape, value.dtype),
        in_specs=[VMEM] * len(operands),
        out_specs=VMEM,
        input_output_aliases={0: 0},
        **settings(cost),
    )(*operands)


def total(top, bottom):
    def kernel(*refs):
        out_ref = refs[-1]
        out_ref[: ROWS["A"]] = sum(ref[...] for ref in refs[1 : len(top)]) + refs[0][...]
        out_ref[ROWS["A"] :] = sum(ref[...] for ref in refs[len(top) + 1 : -1]) + refs[len(top)][...]

    return pl.pallas_call(
        kernel,
        out_shape=jax.ShapeDtypeStruct((TILE, WIDTH), jnp.float32),
        in_specs=[VMEM] * (len(top) + len(bottom)),
        **settings("last"),
    )(*top, *bottom)


def both_cores(value):
    return lax.all_to_all(jnp.broadcast_to(value[None], (2, *value.shape)), "c", 0, 0, tiled=True)


def shards(left, right, left_mask, right_mask, result_mask):
    yl, x, c, yh, z = (lax.axis_index(a) for a in AXES)
    spots = jnp.stack([yl, x, c, yh, z]).astype(jnp.int32)
    masks = (left_mask, right_mask, result_mask)

    here = x // 2 == yl
    across, beside, between = (permute(left, x=bits) for bits in (2, 3, 1))
    right = split(spots, masks, right)
    across, right = lax.optimization_barrier((across, right))
    mine = jnp.stack([jnp.where(here, between, beside), jnp.where(here, left, across)])
    others = jnp.stack([jnp.where(here, beside, between), jnp.where(here, across, left)])
    others = along_y(others, 1)
    p = product(
        (0, 2),
        {
            "y1": [("A", 2, 0)],
            "y3": [("A", 2, 1), ("A", 2, 2), ("A", 2, 3)],
            "z1": [("B", 0, 2), ("B", 0, 1)],
            "z3": [("B", 2, 2), ("B", 2, 3)],
            "z1_kept": [("B", 2, 1)],
            "z3_kept": [("B", 0, 3)],
            "a": [("A", 0, d) for d in range(4)],
            "b": [("B", 0, 0), ("B", 2, 0)],
        },
        spots,
        masks,
        (mine, permute(mine, c=1)),
        right,
        "first",
    )
    from_y1 = along_y(p["y1"], 1)
    from_y3 = along_y(p["y3"], 3)
    from_z1 = along_z(p["z1"], 1)
    from_z3 = along_z(p["z3"], 3)
    others, a_own = lax.optimization_barrier((others, p["a"]))
    others, from_y1 = lax.optimization_barrier((both_cores(others), from_y1))
    q = product(
        (1, 3),
        {
            "y1": [("A", 1, d) for d in range(4)],
            "y3": [("A", 3, d) for d in range(4)],
            "z1": [("B", 1, 2), ("B", 1, 1), ("B", 1, 1)],
            "z3": [("B", 3, 2), ("B", 3, 3), ("B", 3, 3)],
            "z1_last": [("B", 3, 1)],
            "z3_last": [("B", 1, 3)],
            "b": [("B", 1, 0), ("B", 3, 0)],
        },
        spots,
        masks,
        (others,),
        right,
        "second",
    )
    sum_y1 = along_y(join(q["y1"], 1, from_y3, "join_a"), 1)
    sum_y3 = along_y(join(q["y3"], 0, from_y1, "join_a"), 3)
    next_z1 = along_z(join(q["z1"], 2, from_z3, "join_b", p["z1_kept"]), 1)
    next_z3 = along_z(join(q["z3"], 2, from_z1, "join_b", p["z3_kept"]), 3)
    last_z1 = along_z(join(q["z1_last"], 0, next_z3, "join_b"), 1)
    last_z3 = along_z(join(q["z3_last"], 0, next_z1, "join_b"), 3)
    a = [a_own[d] + sum_y1[d] + sum_y3[d] for d in range(4)]
    b = [
        p["b"][0] + from_z1[1] + next_z3[2],
        q["b"][0] + next_z1[1] + last_z3[0],
        p["b"][1] + next_z1[2] + from_z3[1],
        q["b"][1] + last_z1[0] + next_z3[1],
    ]
    return total(
        [a[0], along_z(a[1], 1), along_z(a[3], 3), along_z(a[2], 2)],
        [b[0], along_y(b[1], 1), along_y(b[2], 2), along_y(b[3], 3)],
    )


def solution(mesh):
    torus = Mesh(mesh.devices.reshape(SIZES), AXES)
    in_specs = (
        P("yl", ("yh", "z", "x", "c")),
        P(("yh", "z", "yl"), ("x", "c")),
        P(),
        P(),
        P(),
    )
    return jax.shard_map(
        shards, mesh=torus, in_specs=in_specs, out_specs=P("yl", ("x", "c", "yh", "z")), check_vma=False
    )
```

```python
import jax
import jax.numpy as jnp
from jax import lax
from jax.experimental import pallas as pl
from jax.experimental.pallas import tpu as pltpu
from jax.sharding import Mesh
from jax.sharding import PartitionSpec as P

TILE = 512
WIDTH = 256
AXES = ("yl", "x", "c", "yh", "z")
SIZES = (2, 4, 2, 2, 4)
ROWS = {"A": 256, "B": 256}
COST = {"split": 1, "first": 1, "second": 1, "join_a": 1, "join_b": 1, "last": 1}
SMEM = pl.BlockSpec(memory_space=pltpu.SMEM)
VMEM = pl.BlockSpec(memory_space=pltpu.VMEM)


def permute(value, yl=0, x=0, c=0, yh=0, z=0):
    bits = (((yl * 4 + x) * 2 + c) * 2 + yh) * 4 + z
    return lax.ppermute(value, AXES, [(n, n ^ bits) for n in range(128)])


def along_y(value, bits):
    return permute(value, yl=bits % 2, yh=bits // 2)


def along_z(value, bits):
    return permute(value, z=bits)


def settings(cost):
    size = 48 if cost == "split" else 8
    return dict(
        compiler_params=pltpu.CompilerParams(vmem_limit_bytes=size * 2**20),
        cost_estimate=pl.CostEstimate(flops=1, bytes_accessed=COST[cost], transcendentals=0),
    )


def split_kernel(spots, left_mask, right_mask, result_mask, right, hi_ref, lo_ref, tiles, sems):
    yl, x, c, yh, z = (spots[n] for n in range(5))
    k = (yh * 4 + z) * 2 + yl
    first = (x * 2 + c) * 4

    def block(n):
        chunk = lax.rem(yh + n // 4, 2) * 4 + jnp.bitwise_xor(z, n % 4)
        j = first + lax.div(chunk, 2)
        used = right_mask[k, j] * (left_mask[0, k] * result_mask[0, j] + left_mask[1, k] * result_mask[1, j]) > 0
        where = pl.ds(pl.multiple_of(chunk * WIDTH, WIDTH), WIDTH)
        return used, pltpu.make_async_copy(right.at[:, where], tiles.at[n], sems.at[n])

    for n in range(8):
        used, copy = block(n)

        @pl.when(used)
        def _():
            copy.start()

    for n in range(8):
        used, copy = block(n)

        @pl.when(used)
        def _():
            copy.wait()
            tile = tiles[n]
            hi = tile.astype(jnp.bfloat16)
            hi_ref[n] = hi
            lo_ref[n] = (tile - hi.astype(jnp.float32)).astype(jnp.bfloat16)


def split(spots, masks, right):
    return pl.pallas_call(
        split_kernel,
        out_shape=[jax.ShapeDtypeStruct((8, TILE, WIDTH), jnp.bfloat16)] * 2,
        in_specs=[SMEM] * 4 + [pl.BlockSpec(memory_space=pltpu.HBM)],
        out_specs=[VMEM] * 2,
        scratch_shapes=[pltpu.VMEM((8, TILE, WIDTH), jnp.float32), pltpu.SemaphoreType.DMA((8,))],
        **settings("split"),
    )(spots, *masks, right)


def product_kernel(turns_all, plan, blocks, spots, left_mask, right_mask, result_mask, *rest):
    pieces, right, outs, (hi_ref, lo_ref) = rest[:blocks], rest[blocks : blocks + 2], rest[blocks + 2 : -2], rest[-2:]
    yl, x, c, yh, z = (spots[n] for n in range(5))
    k = (yh * 4 + z) * 2 + yl
    first = (x * 2 + c) * 4
    near = 1 - lax.rem(x, 2)

    def used(dy, chunk):
        i = lax.rem(yl + dy % 2, 2)
        j = first + lax.div(chunk, 2)
        return left_mask[i, k] * right_mask[k, j] * result_mask[i, j] > 0

    groups = [
        (n, lax.rem(yh + high, 2) * 4 + jnp.bitwise_xor(z, dz), [dy for dy in turns_all if dy // 2 == high], dz)
        for n, (high, dz) in enumerate((high, dz) for high in range(2) for dz in range(4))
    ]

    if blocks == 2:
        cores = [(c, pieces[0]), (1 - c, pieces[1])]
    else:
        cores = [(core, pieces[0].at[core]) for core in range(2)]
    for core, piece in cores:
        for n, chip in enumerate((near, 1 - near)):
            value = piece[n]
            hi = value.astype(jnp.bfloat16)
            where = pl.ds(pl.multiple_of(chip * 256 + core * 128, 128), 128)
            hi_ref[:, where] = hi
            lo_ref[:, where] = (value - hi.astype(jnp.float32)).astype(jnp.bfloat16)
    for n, chunk, turns, dz in groups:

        for dy in turns:

            @pl.when(used(dy, chunk))
            def _():
                hi, lo = right[0][n], right[1][n]
                total = jnp.dot(hi_ref[...], hi, preferred_element_type=jnp.float32)
                total += jnp.dot(hi_ref[...], lo, preferred_element_type=jnp.float32)
                total += jnp.dot(lo_ref[...], hi, preferred_element_type=jnp.float32)
                done = 0
                for half, out, slot in plan[dy, dz]:
                    outs[out][slot] = total[done : done + ROWS[half]]
                    done += ROWS[half]

            @pl.when(jnp.logical_not(used(dy, chunk)))
            def _():
                for half, out, slot in plan[dy, dz]:
                    outs[out][slot] = jnp.zeros((ROWS[half], WIDTH), jnp.float32)


def product(turns, names, spots, masks, pieces, right, cost):
    plan = {
        (dy, dz): [
            (half, n, blocks.index((half, dy, dz)))
            for half in "AB"
            for n, blocks in enumerate(names.values())
            if (half, dy, dz) in blocks
        ]
        for dy in turns
        for dz in range(4)
    }
    outs = pl.pallas_call(
        lambda *refs: product_kernel(turns, plan, len(pieces), *refs),
        out_shape=[jax.ShapeDtypeStruct((len(b), ROWS[b[0][0]], WIDTH), jnp.float32) for b in names.values()],
        in_specs=[SMEM] * 4 + [VMEM] * (len(pieces) + 2),
        out_specs=[VMEM] * len(names),
        scratch_shapes=[pltpu.VMEM((TILE, TILE), jnp.bfloat16)] * 2,
        **settings(cost),
    )(spots, *masks, *pieces, *right)
    return dict(zip(names, outs))


def join(value, first, arrived, cost, kept=None):
    def kernel(value_ref, arrived_ref, *rest):
        out_ref = rest[-1]
        del value_ref
        for n in range(count):
            out_ref[first + n] = (rest[0][n] if kept is not None else out_ref[first + n]) + arrived_ref[n]

    count = min(value.shape[0] - first, arrived.shape[0])
    operands = [value, arrived] + ([] if kept is None else [kept])
    return pl.pallas_call(
        kernel,
        out_shape=jax.ShapeDtypeStruct(value.shape, value.dtype),
        in_specs=[VMEM] * len(operands),
        out_specs=VMEM,
        input_output_aliases={0: 0},
        **settings(cost),
    )(*operands)


def total(top, bottom):
    def kernel(*refs):
        out_ref = refs[-1]
        out_ref[: ROWS["A"]] = sum(ref[...] for ref in refs[1 : len(top)]) + refs[0][...]
        out_ref[ROWS["A"] :] = sum(ref[...] for ref in refs[len(top) + 1 : -1]) + refs[len(top)][...]

    return pl.pallas_call(
        kernel,
        out_shape=jax.ShapeDtypeStruct((TILE, WIDTH), jnp.float32),
        in_specs=[VMEM] * (len(top) + len(bottom)),
        **settings("last"),
    )(*top, *bottom)


def both_cores(value):
    return lax.all_to_all(jnp.broadcast_to(value[None], (2, *value.shape)), "c", 0, 0, tiled=True)


def shards(left, right, left_mask, right_mask, result_mask):
    yl, x, c, yh, z = (lax.axis_index(a) for a in AXES)
    spots = jnp.stack([yl, x, c, yh, z]).astype(jnp.int32)
    masks = (left_mask, right_mask, result_mask)

    here = x // 2 == yl
    across, beside, between = (permute(left, x=bits) for bits in (2, 3, 1))
    right = split(spots, masks, right)
    mine = jnp.stack([jnp.where(here, between, beside), jnp.where(here, left, across)])
    others = jnp.stack([jnp.where(here, beside, between), jnp.where(here, across, left)])
    others = along_y(others, 1)
    p = product(
        (0, 2),
        {
            "y1": [("A", 2, 0)],
            "y3": [("A", 2, 1), ("A", 2, 2), ("A", 2, 3)],
            "z1": [("B", 0, 2), ("B", 0, 1)],
            "z3": [("B", 2, 2), ("B", 2, 3)],
            "z1_kept": [("B", 2, 1)],
            "z3_kept": [("B", 0, 3)],
            "a": [("A", 0, d) for d in range(4)],
            "b": [("B", 0, 0), ("B", 2, 0)],
        },
        spots,
        masks,
        (mine, permute(mine, c=1)),
        right,
        "first",
    )
    from_y1 = along_y(p["y1"], 1)
    from_y3 = along_y(p["y3"], 3)
    from_z1 = along_z(p["z1"], 1)
    from_z3 = along_z(p["z3"], 3)
    others, a_own = lax.optimization_barrier((others, p["a"]))
    others, from_y1 = lax.optimization_barrier((both_cores(others), from_y1))
    q = product(
        (1, 3),
        {
            "y1": [("A", 1, d) for d in range(4)],
            "y3": [("A", 3, d) for d in range(4)],
            "z1": [("B", 1, 2), ("B", 1, 1), ("B", 1, 1)],
            "z3": [("B", 3, 2), ("B", 3, 3), ("B", 3, 3)],
            "z1_last": [("B", 3, 1)],
            "z3_last": [("B", 1, 3)],
            "b": [("B", 1, 0), ("B", 3, 0)],
        },
        spots,
        masks,
        (others,),
        right,
        "second",
    )
    sum_y1 = along_y(join(q["y1"], 1, from_y3, "join_a"), 1)
    sum_y3 = along_y(join(q["y3"], 0, from_y1, "join_a"), 3)
    next_z1 = along_z(join(q["z1"], 2, from_z3, "join_b", p["z1_kept"]), 1)
    next_z3 = along_z(join(q["z3"], 2, from_z1, "join_b", p["z3_kept"]), 3)
    last_z1 = along_z(join(q["z1_last"], 0, next_z3, "join_b"), 1)
    last_z3 = along_z(join(q["z3_last"], 0, next_z1, "join_b"), 3)
    a = [a_own[d] + sum_y1[d] + sum_y3[d] for d in range(4)]
    b = [
        p["b"][0] + from_z1[1] + next_z3[2],
        q["b"][0] + next_z1[1] + last_z3[0],
        p["b"][1] + next_z1[2] + from_z3[1],
        q["b"][1] + last_z1[0] + next_z3[1],
    ]
    return total(
        [a[0], along_z(a[1], 1), along_z(a[3], 3), along_z(a[2], 2)],
        [b[0], along_y(b[1], 1), along_y(b[2], 2), along_y(b[3], 3)],
    )


def solution(mesh):
    torus = Mesh(mesh.devices.reshape(SIZES), AXES)
    in_specs = (
        P("yl", ("yh", "z", "x", "c")),
        P(("yh", "z", "yl"), ("x", "c")),
        P(),
        P(),
        P(),
    )
    return jax.shard_map(
        shards, mesh=torus, in_specs=in_specs, out_specs=P("yl", ("x", "c", "yh", "z")), check_vma=False
    )
```

```python
import jax
import jax.numpy as jnp
from jax import lax
from jax.experimental import pallas as pl
from jax.experimental.pallas import tpu as pltpu
from jax.sharding import Mesh
from jax.sharding import PartitionSpec as P

TILE = 512
WIDTH = 256
AXES = ("yl", "x", "c", "yh", "z")
SIZES = (2, 4, 2, 2, 4)
ROWS = {"A": 256, "B": 256}
COST = {"split": 1, "first": 1, "second": 1, "join_a": 1, "join_b": 1, "last": 1}
SMEM = pl.BlockSpec(memory_space=pltpu.SMEM)
VMEM = pl.BlockSpec(memory_space=pltpu.VMEM)


def permute(value, yl=0, x=0, c=0, yh=0, z=0):
    bits = (((yl * 4 + x) * 2 + c) * 2 + yh) * 4 + z
    return lax.ppermute(value, AXES, [(n, n ^ bits) for n in range(128)])


def along_y(value, bits):
    return permute(value, yl=bits % 2, yh=bits // 2)


def along_z(value, bits):
    return permute(value, z=bits)


def settings(cost):
    size = 48 if cost == "split" else 8
    return dict(
        compiler_params=pltpu.CompilerParams(vmem_limit_bytes=size * 2**20),
        cost_estimate=pl.CostEstimate(flops=1, bytes_accessed=COST[cost], transcendentals=0),
    )


def split_kernel(spots, left_mask, right_mask, result_mask, right, hi_ref, lo_ref, tiles, sems):
    yl, x, c, yh, z = (spots[n] for n in range(5))
    k = (yh * 4 + z) * 2 + yl
    first = (x * 2 + c) * 4

    def block(n):
        chunk = lax.rem(yh + n // 4, 2) * 4 + jnp.bitwise_xor(z, n % 4)
        j = first + lax.div(chunk, 2)
        used = right_mask[k, j] * (left_mask[0, k] * result_mask[0, j] + left_mask[1, k] * result_mask[1, j]) > 0
        where = pl.ds(pl.multiple_of(chunk * WIDTH, WIDTH), WIDTH)
        return used, pltpu.make_async_copy(right.at[:, where], tiles.at[n], sems.at[n])

    for n in range(8):
        used, copy = block(n)

        @pl.when(used)
        def _():
            copy.start()

    for n in range(8):
        used, copy = block(n)

        @pl.when(used)
        def _():
            copy.wait()
            tile = tiles[n]
            hi = tile.astype(jnp.bfloat16)
            hi_ref[n] = hi
            lo_ref[n] = (tile - hi.astype(jnp.float32)).astype(jnp.bfloat16)


def split(spots, masks, right):
    return pl.pallas_call(
        split_kernel,
        out_shape=[jax.ShapeDtypeStruct((8, TILE, WIDTH), jnp.bfloat16)] * 2,
        in_specs=[SMEM] * 4 + [pl.BlockSpec(memory_space=pltpu.HBM)],
        out_specs=[VMEM] * 2,
        scratch_shapes=[pltpu.VMEM((8, TILE, WIDTH), jnp.float32), pltpu.SemaphoreType.DMA((8,))],
        **settings("split"),
    )(spots, *masks, right)


def product_kernel(turns_all, plan, blocks, spots, left_mask, right_mask, result_mask, *rest):
    pieces, right, outs, (hi_ref, lo_ref) = rest[:blocks], rest[blocks : blocks + 2], rest[blocks + 2 : -2], rest[-2:]
    yl, x, c, yh, z = (spots[n] for n in range(5))
    k = (yh * 4 + z) * 2 + yl
    first = (x * 2 + c) * 4
    near = 1 - lax.rem(x, 2)

    def used(dy, chunk):
        i = lax.rem(yl + dy % 2, 2)
        j = first + lax.div(chunk, 2)
        return left_mask[i, k] * right_mask[k, j] * result_mask[i, j] > 0

    groups = [
        (n, lax.rem(yh + high, 2) * 4 + jnp.bitwise_xor(z, dz), [dy for dy in turns_all if dy // 2 == high], dz)
        for n, (high, dz) in enumerate((high, dz) for high in range(2) for dz in range(4))
    ]

    if blocks == 2:
        cores = [(c, pieces[0]), (1 - c, pieces[1])]
    else:
        cores = [(core, pieces[0].at[core]) for core in range(2)]
    for core, piece in cores:
        for n, chip in enumerate((near, 1 - near)):
            value = piece[n]
            hi = value.astype(jnp.bfloat16)
            where = pl.ds(pl.multiple_of(chip * 256 + core * 128, 128), 128)
            hi_ref[:, where] = hi
            lo_ref[:, where] = (value - hi.astype(jnp.float32)).astype(jnp.bfloat16)
    for n, chunk, turns, dz in groups:

        for dy in turns:

            @pl.when(used(dy, chunk))
            def _():
                hi, lo = right[0][n], right[1][n]
                total = jnp.dot(hi_ref[...], hi, preferred_element_type=jnp.float32)
                total += jnp.dot(hi_ref[...], lo, preferred_element_type=jnp.float32)
                total += jnp.dot(lo_ref[...], hi, preferred_element_type=jnp.float32)
                done = 0
                for half, out, slot in plan[dy, dz]:
                    outs[out][slot] = total[done : done + ROWS[half]]
                    done += ROWS[half]

            @pl.when(jnp.logical_not(used(dy, chunk)))
            def _():
                for half, out, slot in plan[dy, dz]:
                    outs[out][slot] = jnp.zeros((ROWS[half], WIDTH), jnp.float32)


def product(turns, names, spots, masks, pieces, right, cost):
    plan = {
        (dy, dz): [
            (half, n, blocks.index((half, dy, dz)))
            for half in "AB"
            for n, blocks in enumerate(names.values())
            if (half, dy, dz) in blocks
        ]
        for dy in turns
        for dz in range(4)
    }
    outs = pl.pallas_call(
        lambda *refs: product_kernel(turns, plan, len(pieces), *refs),
        out_shape=[jax.ShapeDtypeStruct((len(b), ROWS[b[0][0]], WIDTH), jnp.float32) for b in names.values()],
        in_specs=[SMEM] * 4 + [VMEM] * (len(pieces) + 2),
        out_specs=[VMEM] * len(names),
        scratch_shapes=[pltpu.VMEM((TILE, TILE), jnp.bfloat16)] * 2,
        **settings(cost),
    )(spots, *masks, *pieces, *right)
    return dict(zip(names, outs))


def join(value, first, arrived, cost, kept=None):
    def kernel(value_ref, arrived_ref, *rest):
        out_ref = rest[-1]
        del value_ref
        for n in range(count):
            out_ref[first + n] = (rest[0][n] if kept is not None else out_ref[first + n]) + arrived_ref[n]

    count = min(value.shape[0] - first, arrived.shape[0])
    operands = [value, arrived] + ([] if kept is None else [kept])
    return pl.pallas_call(
        kernel,
        out_shape=jax.ShapeDtypeStruct(value.shape, value.dtype),
        in_specs=[VMEM] * len(operands),
        out_specs=VMEM,
        input_output_aliases={0: 0},
        **settings(cost),
    )(*operands)


def total(top, bottom):
    def kernel(*refs):
        out_ref = refs[-1]
        out_ref[: ROWS["A"]] = sum(ref[...] for ref in refs[1 : len(top)]) + refs[0][...]
        out_ref[ROWS["A"] :] = sum(ref[...] for ref in refs[len(top) + 1 : -1]) + refs[len(top)][...]

    return pl.pallas_call(
        kernel,
        out_shape=jax.ShapeDtypeStruct((TILE, WIDTH), jnp.float32),
        in_specs=[VMEM] * (len(top) + len(bottom)),
        **settings("last"),
    )(*top, *bottom)


def both_cores(value):
    return lax.all_to_all(jnp.broadcast_to(value[None], (2, *value.shape)), "c", 0, 0, tiled=True)


def shards(left, right, left_mask, right_mask, result_mask):
    yl, x, c, yh, z = (lax.axis_index(a) for a in AXES)
    spots = jnp.stack([yl, x, c, yh, z]).astype(jnp.int32)
    masks = (left_mask, right_mask, result_mask)

    here = x // 2 == yl
    across, beside, between = (permute(left, x=bits) for bits in (2, 3, 1))
    right = split(spots, masks, right)
    mine = jnp.stack([jnp.where(here, between, beside), jnp.where(here, left, across)])
    others = jnp.stack([jnp.where(here, beside, between), jnp.where(here, across, left)])
    others = along_y(others, 1)
    p = product(
        (0, 2),
        {
            "y1": [("A", 2, 0)],
            "y3": [("A", 2, 1), ("A", 2, 2), ("A", 2, 3)],
            "z1": [("B", 0, 2), ("B", 0, 1)],
            "z3": [("B", 2, 2), ("B", 2, 3)],
            "z1_kept": [("B", 2, 1)],
            "z3_kept": [("B", 0, 3)],
            "a": [("A", 0, d) for d in range(4)],
            "b": [("B", 0, 0), ("B", 2, 0)],
        },
        spots,
        masks,
        (mine, permute(mine, c=1)),
        right,
        "first",
    )
    from_y1 = along_y(p["y1"], 1)
    from_y3 = along_y(p["y3"], 3)
    from_z1 = along_z(p["z1"], 1)
    from_z3 = along_z(p["z3"], 3)
    others, a_own = lax.optimization_barrier((others, p["a"]))
    others, from_y1 = lax.optimization_barrier((both_cores(others), from_y1))
    q = product(
        (1, 3),
        {
            "y1": [("A", 1, d) for d in range(4)],
            "y3": [("A", 3, d) for d in range(4)],
            "z1": [("B", 1, 2), ("B", 1, 1), ("B", 1, 1)],
            "z3": [("B", 3, 2), ("B", 3, 3), ("B", 3, 3)],
            "z1_last": [("B", 3, 1)],
            "z3_last": [("B", 1, 3)],
            "b": [("B", 1, 0), ("B", 3, 0)],
        },
        spots,
        masks,
        (others,),
        right,
        "second",
    )
    sum_y1 = along_y(join(q["y1"], 1, from_y3, "join_a"), 1)
    sum_y3 = along_y(join(q["y3"], 0, from_y1, "join_a"), 3)
    next_z1 = along_z(join(q["z1"], 2, from_z3, "join_b", p["z1_kept"]), 1)
    next_z3 = along_z(join(q["z3"], 2, from_z1, "join_b", p["z3_kept"]), 3)
    last_z1 = along_z(join(q["z1_last"], 0, next_z3, "join_b"), 1)
    last_z3 = along_z(join(q["z3_last"], 0, next_z1, "join_b"), 3)
    a = [a_own[d] + sum_y1[d] + sum_y3[d] for d in range(4)]
    b = [
        p["b"][0] + from_z1[1] + next_z3[2],
        q["b"][0] + next_z1[1] + last_z3[0],
        p["b"][1] + next_z1[2] + from_z3[1],
        q["b"][1] + last_z1[0] + next_z3[1],
    ]
    return total(
        [a[0], along_z(a[1], 1), along_z(a[3], 3), along_z(a[2], 2)],
        [b[0], along_y(b[3], 3), along_y(b[1], 1), along_y(b[2], 2)],
    )


def solution(mesh):
    torus = Mesh(mesh.devices.reshape(SIZES), AXES)
    in_specs = (
        P("yl", ("yh", "z", "x", "c")),
        P(("yh", "z", "yl"), ("x", "c")),
        P(),
        P(),
        P(),
    )
    return jax.shard_map(
        shards, mesh=torus, in_specs=in_specs, out_specs=P("yl", ("x", "c", "yh", "z")), check_vma=False
    )
```
